768 devices in a mesh: gx: 96 (over z, x, core), yz: 8 (over y).
Axes of the slice: x: 4, y: 8, z: 12, core: 2. Of those that a mesh axis runs over, the one named last changes fastest.
Arguments:
- coarse_state: float32 [21, 576, 48, 384], P(None, 'gx', 'yz')
- fine_state: bfloat16 [6144, 21, 512], P(('gx', 'yz')), may hold values from -6 to 6
- diffusion: float32 [21], replicated, may hold values from 0.005 to 0.04
- rate: float32 [21, 21], replicated, may hold values from -0.625 to 0.625
- box_pos: int32 [96, 8, 4], P('gx', 'yz'), may hold values from 0 to 63, as said below
- box_owner: int32 [96, 8, 4], P('gx', 'yz'), may hold values from 0 to 7, as said below
Outputs:
- coarse_next: float32 [21, 576, 48, 384], P(None, 'gx', 'yz')
- fine_next: bfloat16 [6144, 21, 512], P(('gx', 'yz'))
The draws below stay inside these ranges and needn't reach their ends.
Inputs may be any that keep to these rules, and one draw needn't show every extreme that they name: `box_pos`: the 4 positions of one device are distinct. `box_owner`: the 4 boxes of one device go to distinct owners of its slab; in every slab some owner receives a box from every device of the slab.
All inputs are finite; a program needn't handle non-finite values.
Results may differ from the reference program's by a relative error of at most 0.0025.
Values may be sent and summed in bfloat16 or wider, within the bound.
A program may use at most 64 MiB of HBM per device.

```python
import math
import jax
import jax.numpy as jnp
from jax import lax

S = 21
PZ = 64
CX = 6
NX = 576
NY = 48
NZ = 384
HB = 4
FC = 512
SLOTS = 6144
N_GX = 96
N_YZ = 8


def draw_coarse_state(key, part):
    key = jax.random.fold_in(key, 5)
    first = jax.random.fold_in(key, 0)
    return jax.random.normal(first, (S, NX, NY, NZ), jnp.float32)


def draw_box_pos(key, part):
    key = jax.random.fold_in(key, 11)
    keys = jax.random.split(key, N_GX * N_YZ)
    picks = jax.vmap(lambda k: jax.random.permutation(k, PZ)[:HB])(keys)
    return picks.reshape(N_GX, N_YZ, HB).astype(jnp.int32)


def owner_row(key, hot):
    first, second = jax.random.split(key)
    others = (hot + 1 + jax.random.permutation(first, N_YZ - 1)[:HB - 1]) % N_YZ
    row = jnp.concatenate([hot[None], others.astype(jnp.int32)])
    return row[jax.random.permutation(second, HB)]


def draw_box_owner(key, part):
    key = jax.random.fold_in(key, 12)
    first, second = jax.random.split(key)
    hot = jax.random.randint(first, (N_GX,), 0, N_YZ).astype(jnp.int32)
    keys = jax.random.split(second, N_GX * N_YZ)
    hots = jnp.repeat(hot, N_YZ)
    rows = jax.vmap(owner_row)(keys, hots)
    return rows.reshape(N_GX, N_YZ, HB).astype(jnp.int32)


def steps_of(key, shape, cuts, low, largest):
    loudness = 1.0
    for axis_at, blocks in cuts:
        steps = jax.random.uniform(jax.random.fold_in(jax.random.fold_in(key, 6), axis_at), (blocks,), jnp.float32, low / len(cuts), largest / len(cuts))
        loudness = loudness * jnp.repeat(jnp.exp(steps), shape[axis_at] // blocks).reshape((-1,) + (1,) * (len(shape) - 1 - axis_at))
    return loudness


def gaussian(own_key, extent, width, bound, shards=(), kind=jnp.bfloat16):
    loudness = steps_of(own_key, extent, shards, -0.22, 0.18) if shards else 1.0
    values = jax.random.normal(own_key, extent, jnp.float32) * width * loudness
    return jnp.minimum(jnp.maximum(values, -bound), bound).astype(kind)


def setup_inputs(seed: int = 0) -> dict:
    streams_of = jax.random.split(jax.random.key(seed), 7)
    coarse_state = draw_coarse_state(jax.random.fold_in(streams_of[6], 71), 0)
    fine_state = gaussian(streams_of[1], (SLOTS, S, FC), 1.0, 6.0, ((0, 768),))
    diffusion = jnp.clip(jnp.exp(jax.random.uniform(streams_of[2], (S,), jnp.float32, math.log(0.005), math.log(0.04))), 0.005, 0.04)
    rate = gaussian(streams_of[3], (S, S), (4 * S) ** -0.5, 0.625, (), jnp.float32)
    box_pos = draw_box_pos(jax.random.fold_in(streams_of[6], 71), 0)
    box_owner = draw_box_owner(jax.random.fold_in(streams_of[6], 71), 0)
    return {"coarse_state": coarse_state, "fine_state": fine_state, "diffusion": diffusion, "rate": rate, "box_pos": box_pos, "box_owner": box_owner}


def react(rate, field):
    return jnp.einsum("st,txyz->sxyz", rate, field, precision=lax.Precision.HIGHEST)


def cycle_faces(patch):
    return jnp.stack([patch[:, 0, 1:-1, 1:-1], patch[:, -1, 1:-1, 1:-1], patch[:, 1:-1, 0, 1:-1], patch[:, 1:-1, -1, 1:-1], patch[:, 1:-1, 1:-1, 0], patch[:, 1:-1, 1:-1, -1]], axis=1)


def inner_faces(patch):
    return jnp.stack([patch[:, 1, 1:-1, 1:-1], patch[:, -2, 1:-1, 1:-1], patch[:, 1:-1, 1, 1:-1], patch[:, 1:-1, -2, 1:-1], patch[:, 1:-1, 1:-1, 1], patch[:, 1:-1, 1:-1, -2]], axis=1)


def widen(face):
    return jnp.repeat(jnp.repeat(face, 2, axis=1), 2, axis=2)


def fine_box(fine, ghost_old, ghost_new, diffusion, rate):
    species = fine.shape[0]
    half = ghost_old.shape[2]
    edge = 2 * half
    field = fine.reshape(species, edge, edge, edge)
    coef = diffusion[:, None, None, None]
    flux_sum = jnp.zeros_like(ghost_old)
    for sub in range(2):
        ghost = ghost_old if sub == 0 else 0.5 * (ghost_old + ghost_new)
        padded = jnp.pad(field, ((0, 0), (1, 1), (1, 1), (1, 1)))
        padded = padded.at[:, 0, 1:-1, 1:-1].set(widen(ghost[:, 0]))
        padded = padded.at[:, -1, 1:-1, 1:-1].set(widen(ghost[:, 1]))
        padded = padded.at[:, 1:-1, 0, 1:-1].set(widen(ghost[:, 2]))
        padded = padded.at[:, 1:-1, -1, 1:-1].set(widen(ghost[:, 3]))
        padded = padded.at[:, 1:-1, 1:-1, 0].set(widen(ghost[:, 4]))
        padded = padded.at[:, 1:-1, 1:-1, -1].set(widen(ghost[:, 5]))
        lap = padded[:, 2:, 1:-1, 1:-1] + padded[:, :-2, 1:-1, 1:-1]
        lap = lap + padded[:, 1:-1, 2:, 1:-1] + padded[:, 1:-1, :-2, 1:-1]
        lap = lap + padded[:, 1:-1, 1:-1, 2:] + padded[:, 1:-1, 1:-1, :-2] - 6.0 * field
        bounds = jnp.stack([field[:, 0], field[:, -1], field[:, :, 0], field[:, :, -1], field[:, :, :, 0], field[:, :, :, -1]], axis=1)
        pooled = bounds.reshape(species, 6, half, 2, half, 2).sum(axis=(3, 5))
        flux_sum = flux_sum + coef * (ghost - 0.25 * pooled)
        field = field + 2.0 * coef * lap + 0.5 * react(rate, field)
    average = field.reshape(species, half, 2, half, 2, half, 2).mean(axis=(2, 4, 6))
    return field.reshape(species, edge * edge * edge), flux_sum, average


def correct(patch_new, patch_old, flux_sum, average, diffusion):
    fix = diffusion[:, None, None, None] * (cycle_faces(patch_old) - inner_faces(patch_old)) - flux_sum
    out = patch_new.at[:, 0, 1:-1, 1:-1].add(fix[:, 0])
    out = out.at[:, -1, 1:-1, 1:-1].add(fix[:, 1])
    out = out.at[:, 1:-1, 0, 1:-1].add(fix[:, 2])
    out = out.at[:, 1:-1, -1, 1:-1].add(fix[:, 3])
    out = out.at[:, 1:-1, 1:-1, 0].add(fix[:, 4])
    out = out.at[:, 1:-1, 1:-1, -1].add(fix[:, 5])
    return out.at[:, 1:-1, 1:-1, 1:-1].set(average)


def reference(coarse_state, fine_state, diffusion, rate, box_pos, box_owner):
    coef = diffusion[:, None, None, None]
    lap = jnp.roll(coarse_state, 1, 1) + jnp.roll(coarse_state, -1, 1)
    lap = lap + jnp.roll(coarse_state, 1, 2) + jnp.roll(coarse_state, -1, 2)
    lap = lap + jnp.roll(coarse_state, 1, 3) + jnp.roll(coarse_state, -1, 3) - 6.0 * coarse_state
    advanced = coarse_state + coef * lap + react(rate, coarse_state)
    zero = jnp.zeros((), jnp.int32)

    def visit(carry, index):
        corrected, fine_out = carry
        slab = (index // (N_YZ * HB)).astype(jnp.int32)
        host = ((index // HB) % N_YZ).astype(jnp.int32)
        which = (index % HB).astype(jnp.int32)
        place = box_pos[slab, host, which].astype(jnp.int32)
        owner = box_owner[slab, host, which].astype(jnp.int32)
        corner = (zero, (slab * CX).astype(jnp.int32), (host * CX).astype(jnp.int32), (place * CX).astype(jnp.int32))
        old = lax.dynamic_slice(coarse_state, corner, (S, CX, CX, CX))
        new = lax.dynamic_slice(advanced, corner, (S, CX, CX, CX))
        slot = ((slab * N_YZ + owner) * N_YZ + host).astype(jnp.int32)
        fine = lax.dynamic_index_in_dim(fine_state, slot, 0, keepdims=False).astype(jnp.float32)
        field, flux_sum, average = fine_box(fine, cycle_faces(old), cycle_faces(new), diffusion, rate)
        corrected = lax.dynamic_update_slice(corrected, correct(new, old, flux_sum, average, diffusion), corner)
        fine_out = lax.dynamic_update_slice(fine_out, field.astype(jnp.bfloat16)[None], (slot, zero, zero))
        return (corrected, fine_out), None

    start = (advanced, jnp.zeros((SLOTS, S, FC), jnp.bfloat16))
    (coarse_next, fine_next), _ = lax.scan(visit, start, jnp.arange(N_GX * N_YZ * HB, dtype=jnp.int32))
    return coarse_next, fine_next
```

```python
import functools

import jax
import jax.numpy as jnp
import numpy as np
from jax import lax
from jax.experimental import pallas as pl
from jax.experimental.pallas import tpu as pltpu
from jax.sharding import PartitionSpec as P

S = 21
BF = jnp.bfloat16
F32 = jnp.float32
SP = 24
ROWS = 6 * SP
NZ = 384
PATCH = 384
FINE = 512
WIDE = 4 * SP


def constants():
    fine = [(x, y, z) for x in range(8) for y in range(8) for z in range(8)]
    touch = np.zeros((PATCH, FINE), np.float32)
    lap = np.zeros((FINE, FINE), np.float32)
    mean = np.zeros((FINE, PATCH), np.float32)
    for cell, at in enumerate(fine):
        lap[cell, cell] = -6.0
        inner = [c // 2 + 1 for c in at]
        mean[cell, inner[0] * 64 + inner[1] * 8 + inner[2]] = 0.125
        for axis, stride in enumerate((64, 8, 1)):
            for step, edge, ghost in ((-1, 0, 0), (1, 7, 5)):
                if at[axis] == edge:
                    cyc = list(inner)
                    cyc[axis] = ghost
                    touch[cyc[0] * 64 + cyc[1] * 8 + cyc[2], cell] = 1.0
                else:
                    lap[cell + step * stride, cell] = 1.0
    face = np.zeros((PATCH, PATCH), np.float32)
    for a in range(1, 5):
        for b in range(1, 5):
            for axis in range(3):
                for low, inner in ((0, 1), (5, 4)):
                    at = [a, b]
                    at.insert(axis, low)
                    near = [a, b]
                    near.insert(axis, inner)
                    q = at[0] * 64 + at[1] * 8 + at[2]
                    face[q, q] = 1.0
                    face[near[0] * 64 + near[1] * 8 + near[2], q] = -1.0
    lap_pool = np.concatenate([lap, 0.25 * touch.T], axis=1)
    return (lap_pool, touch, mean, face)


def iota(shape, dim):
    return lax.broadcasted_iota(jnp.int32, shape, dim)


def dot(a, b):
    return jnp.dot(a, b, preferred_element_type=F32)


def one(mask, kind=BF):
    return jnp.where(mask, 1.0, 0.0).astype(kind)


def split(value):
    high = value.astype(BF)
    return high, (value - high.astype(F32)).astype(BF)


def kernel(
    n_gx,
    n_yz,
    coarse,
    fine,
    diffusion,
    rate,
    box_pos,
    box_owner,
    lap_pool_in,
    touch_in,
    mean_in,
    face_in,
    coarse_out,
    fine_out,
    cv,
    fv,
    lap_pool,
    touch,
    mean,
    face,
    rz,
    xf,
    xh,
    adv,
    ysend,
    yrecv,
    xrecv,
    packed,
    fbuf,
    sbuf,
    rbuf,
    ov,
    load_sem,
    own_sem,
    halo_send,
    halo_recv,
    fine_send,
    fine_recv,
    back_send,
    back_recv,
    out_sem,
):
    gx = lax.axis_index("gx")
    me = lax.axis_index("yz")
    right, left = lax.rem(gx + 1, n_gx), lax.rem(gx + n_gx - 1, n_gx)
    up, down = lax.rem(me + 1, n_yz), lax.rem(me + n_yz - 1, n_yz)
    mesh_id = pl.DeviceIdType.MESH

    loads = [
        pltpu.make_async_copy(coarse, cv, load_sem.at[0]),
        pltpu.make_async_copy(fine, fv, load_sem.at[1]),
        pltpu.make_async_copy(lap_pool_in, lap_pool, load_sem.at[2]),
        pltpu.make_async_copy(touch_in, touch, load_sem.at[3]),
        pltpu.make_async_copy(mean_in, mean, load_sem.at[4]),
        pltpu.make_async_copy(face_in, face, load_sem.at[5]),
    ]
    for copy in loads:
        copy.start()

    barrier = pltpu.get_barrier_semaphore()
    for step in range(1, n_yz):
        pl.semaphore_signal(
            barrier, inc=1, device_id=(gx, lax.rem(me + step, n_yz)), device_id_type=mesh_id
        )
    for other in (left, right):
        pl.semaphore_signal(barrier, inc=1, device_id=(other, me), device_id_type=mesh_id)

    loads[0].wait()
    for x in range(6):
        value = jnp.concatenate([cv[x], jnp.zeros((6, SP - S, NZ), F32)], axis=1)
        value = value.reshape(ROWS, NZ)
        xf[x] = value
        xh[x] = value.astype(BF)
        if x % 2:
            before = xf[x - 1]
            first = jnp.concatenate([before[:SP], value[:SP]], axis=0)
            last = jnp.concatenate([before[ROWS - SP :], value[ROWS - SP :]], axis=0)
            ysend[0, x // 2] = first.astype(BF)
            ysend[1, x // 2] = last.astype(BF)

    loads[1].wait()
    slots = fv[...].astype(F32).reshape(S * 8, FINE)
    slots = jnp.concatenate([slots, jnp.zeros((8, FINE), F32)], axis=0).astype(BF)
    row = iota((8, SP, S * 8 + 8), 1) * 8 + iota((8, SP, S * 8 + 8), 0)
    order = one(row == iota((8, SP, S * 8 + 8), 2), F32).reshape(8 * SP, S * 8 + 8)
    slots = dot(order.astype(BF), slots)
    for j in range(8):
        value = slots[j * SP : (j + 1) * SP]
        value = jnp.concatenate([value[:, : FINE // 2], value[:, FINE // 2 :]], axis=0)
        packed[j] = value.astype(BF)

    pl.semaphore_wait(barrier, n_yz + 1)

    def remote(src, dst, sends, recvs, at, target):
        return pltpu.make_async_remote_copy(
            src_ref=src,
            dst_ref=dst,
            send_sem=sends.at[at],
            recv_sem=recvs.at[at],
            device_id=target,
            device_id_type=mesh_id,
        )

    halos = [
        remote(ysend.at[0], yrecv.at[1], halo_send, halo_recv, 0, (gx, down)),
        remote(ysend.at[1], yrecv.at[0], halo_send, halo_recv, 1, (gx, up)),
        remote(xh.at[0], xrecv.at[1], halo_send, halo_recv, 2, (left, me)),
        remote(xh.at[5], xrecv.at[0], halo_send, halo_recv, 3, (right, me)),
    ]
    for copy in halos:
        copy.start()
    gathers = []
    for step in (4, 3, 5, 2, 6, 1, 7):
        host = lax.rem(me + step, n_yz)
        gathers.append(
            remote(packed.at[host], fbuf.at[me], fine_send, fine_recv, step, (gx, host))
        )
        gathers[-1].start()
    mine = pltpu.make_async_copy(packed.at[me], fbuf.at[me], own_sem.at[0])
    mine.start()

    rz[...] = jnp.zeros_like(rz)
    rz[0:S, 0:S] = rate[...]
    rate_high, rate_low = split(rz[...])

    def repeated(count):
        at = iota((count, SP, 128), 1)
        return one(at == iota((count, SP, 128), 2), F32).reshape(count * SP, 128).astype(BF)

    def group(count):
        return iota((count, SP, 1), 0).astype(F32).reshape(count * SP, 1)

    def group_lane(count):
        lane = iota((1, count * SP), 1)
        at = jnp.zeros((1, count * SP), jnp.int32)
        for i in range(1, count):
            at = at + jnp.where(lane >= i * SP, 1, 0)
        return at.astype(F32)

    def blocks(count, part):
        tall = repeated(count)
        full = lax.dot_general(
            dot(tall, part).astype(BF), tall, (((1,), (1,)), ((), ())), preferred_element_type=F32
        )
        return jnp.where(group(count) == group_lane(count), full, 0.0)

    mix_high = blocks(6, rate_high).astype(BF)
    mix_low = blocks(6, rate_low).astype(BF)
    box_high = (0.5 * blocks(4, rate_high)).astype(BF)
    box_low = (0.5 * blocks(4, rate_low)).astype(BF)
    at = iota((SP, 1), 0)
    column = jnp.zeros((SP, 1), F32)
    for s in range(S):
        column = jnp.where(at == s, diffusion[s], column)
    d_slab = jnp.concatenate([column] * 6, axis=0)
    d_box = jnp.concatenate([column] * 4, axis=0)

    def start_of(index):
        place = jnp.full(index.shape, box_pos[0, 0, 0] * 6, jnp.int32)
        for i in range(1, 4):
            place = jnp.where(index == i, box_pos[0, 0, i] * 6, place)
        return place

    lane = iota((1, 256), 1)
    want = jnp.where((lane & 7) < 6, start_of(lane >> 6) + (lane & 7), -1)
    take = one(iota((NZ, 256), 0) == want)
    lane = iota((256, 1), 0)
    want = jnp.where((lane & 7) < 6, start_of(lane >> 6) + (lane & 7), -1)
    give = one(iota((256, NZ), 1) == want)
    y_lane = (iota((1, 256), 1) >> 3) & 7

    def to_patch(slab):
        cells = dot(slab, take)
        patch = jnp.zeros((SP, 256), F32)
        for y in range(6):
            patch = jnp.where(y_lane == y, cells[y * SP : (y + 1) * SP], patch)
        return patch

    def by_box(parts):
        rows = [
            jnp.concatenate([part[:, i * 64 : (i + 1) * 64] for part in parts], axis=1)
            for i in range(4)
        ]
        return jnp.concatenate(rows, axis=0)

    olds = []
    for x in range(6):
        value = xf[x]
        high = xh[x]
        low = (value - high.astype(F32)).astype(BF)
        around = pltpu.roll(value, 1, 1) + pltpu.roll(value, NZ - 1, 1) - 6.0 * value
        if x > 0:
            around = around + xf[x - 1]
        if x < 5:
            around = around + xf[x + 1]
        rest = jnp.zeros((SP, NZ), F32)
        around = around + jnp.concatenate([rest, value[: ROWS - SP]], axis=0)
        around = around + jnp.concatenate([value[SP:], rest], axis=0)
        mixed = dot(mix_high, high) + dot(mix_low, high) + dot(mix_high, low)
        adv[x] = value + mixed + d_slab * around
        olds.append(to_patch(high))
    old = by_box(olds)

    for copy in halos:
        copy.wait_recv()
    news = []
    rest = jnp.zeros((ROWS - 2 * SP, NZ), F32)
    for pair in range(3):
        before = yrecv[0, pair].astype(F32)
        after = yrecv[1, pair].astype(F32)
        for k in range(2):
            x = 2 * pair + k
            part = slice(k * SP, (k + 1) * SP)
            around = jnp.concatenate([before[part], rest, after[part]], axis=0)
            if x == 0:
                around = around + xrecv[0].astype(F32)
            if x == 5:
                around = around + xrecv[1].astype(F32)
            value = adv[x] + d_slab * around
            adv[x] = value
            news.append(to_patch(value.astype(BF)))
    new = by_box(news)

    for copy in loads[2:]:
        copy.wait()
    ghost_old = dot(old.astype(BF), touch[...])
    ghost_mid = 0.5 * (ghost_old + dot(new.astype(BF), touch[...]))
    for copy in gathers:
        copy.wait_recv()
    mine.wait()
    boxes = []
    for i in range(4):
        value = fbuf[box_owner[0, 0, i]].astype(F32)
        boxes.append(jnp.concatenate([value[:SP], value[SP:]], axis=1))
    field = jnp.concatenate(boxes, axis=0)
    high = field.astype(BF)
    both = dot(high, lap_pool[...])
    pooled = both[:, FINE:]
    field = (
        field
        + (2.0 * d_box) * (both[:, :FINE] + ghost_old)
        + (dot(box_high, high) + dot(box_low, high))
    )
    high, low = split(field)
    both = dot(high, lap_pool[...]) + dot(low, lap_pool[...])
    pooled = pooled + both[:, FINE:]
    field = (
        field
        + (2.0 * d_box) * (both[:, :FINE] + ghost_mid)
        + (dot(box_high, high) + dot(box_low, high) + dot(box_high, low))
    )

    for owner in range(8):
        slot = jnp.zeros((SP, FINE), F32)
        for i in range(4):
            sent = box_owner[0, 0, i] == owner
            slot = slot + jnp.where(sent, field[i * SP : (i + 1) * SP], 0.0)
        slot = jnp.concatenate([slot[:, : FINE // 2], slot[:, FINE // 2 :]], axis=0)
        sbuf[owner] = slot.astype(BF)
    backs = []
    for step in (4, 3, 5, 2, 6, 1, 7):
        owner = lax.rem(me + step, n_yz)
        backs.append(
            remote(sbuf.at[owner], rbuf.at[me], back_send, back_recv, step, (gx, owner))
        )
        backs[-1].start()
    own = pltpu.make_async_copy(sbuf.at[me], rbuf.at[me], own_sem.at[1])
    own.start()

    lane = iota((1, PATCH), 1)
    parts = [(lane >> 6), (lane >> 3) & 7, lane & 7]
    ends = [jnp.where((part == 0) | (part == 5), 1, 0) for part in parts]
    outside = [jnp.where(part > 5, 1, 0) for part in parts]
    on_face = (ends[0] + ends[1] + ends[2] == 1) & (outside[0] + outside[1] + outside[2] == 0)
    ghosts = jnp.where(on_face, 1.5 * old + 0.5 * new, 0.0)
    delta = d_box * (dot(old.astype(BF), face[...]) - ghosts + pooled)
    delta = delta + dot(field.astype(BF), mean[...])
    zat = iota((1, NZ), 1)
    inside = jnp.zeros((1, NZ), jnp.int32)
    for i in range(4):
        offset = zat - box_pos[0, 0, i] * 6
        inside = inside + jnp.where((offset >= 1) & (offset <= 4), 1, 0)
    stores = []
    for x in range(6):
        part = [delta[i * SP : (i + 1) * SP, x * 64 : (x + 1) * 64] for i in range(4)]
        part = jnp.concatenate(part, axis=1)
        cells = [jnp.where(y_lane == y, part, 0.0) for y in range(6)]
        change = dot(jnp.concatenate(cells, axis=0).astype(BF), give)
        value = adv[x]
        total = value + change
        if 1 <= x <= 4:
            middle = jnp.where(inside > 0, change[SP : ROWS - SP], total[SP : ROWS - SP])
            total = jnp.concatenate([total[:SP], middle, total[ROWS - SP :]], axis=0)
        ov[x] = total.reshape(6, SP, NZ)[:, :S]
        stores.append(pltpu.make_async_copy(ov.at[x], coarse_out.at[x], out_sem.at[x]))
        stores[-1].start()

    row = iota((S, 8, 8 * SP), 1) * SP + iota((S, 8, 8 * SP), 0)
    order = one(row == iota((S, 8, 8 * SP), 2), F32).reshape(S * 8, 8 * SP).astype(BF)
    for copy in backs:
        copy.wait_recv()
    own.wait()
    slots = []
    for j in range(8):
        value = rbuf[j].astype(F32)
        slots.append(jnp.concatenate([value[:SP], value[SP:]], axis=1))
    slots = jnp.concatenate(slots, axis=0).astype(BF)
    fine_out[...] = dot(order, slots).reshape(S, 8, FINE).astype(BF)

    for copy in halos + gathers + backs:
        copy.wait_send()
    for copy in stores:
        copy.wait()


def local(n_gx, n_yz, consts, coarse_state, fine_state, diffusion, rate, box_pos, box_owner):
    hbm = pl.BlockSpec(memory_space=pl.ANY)
    vmem = pl.BlockSpec(memory_space=pltpu.VMEM)
    smem = pl.BlockSpec(memory_space=pltpu.SMEM)
    dma = pltpu.SemaphoreType.DMA
    coarse, fine = pl.pallas_call(
        functools.partial(kernel, n_gx, n_yz),
        out_shape=(
            jax.ShapeDtypeStruct((6, 6, S, NZ), F32),
            jax.ShapeDtypeStruct((S, 8, FINE), BF),
        ),
        in_specs=[hbm, hbm, smem, vmem, smem, smem, hbm, hbm, hbm, hbm],
        out_specs=(hbm, vmem),
        scratch_shapes=[
            pltpu.VMEM((6, 6, S, NZ), F32),
            pltpu.VMEM((S, 8, FINE), BF),
            pltpu.VMEM((FINE, FINE + PATCH), BF),
            pltpu.VMEM((PATCH, FINE), BF),
            pltpu.VMEM((FINE, PATCH), BF),
            pltpu.VMEM((PATCH, PATCH), BF),
            pltpu.VMEM((128, 128), F32),
            pltpu.VMEM((6, ROWS, NZ), F32),
            pltpu.VMEM((6, ROWS, NZ), BF),
            pltpu.VMEM((6, ROWS, NZ), F32),
            pltpu.VMEM((2, 3, 2 * SP, NZ), BF),
            pltpu.VMEM((2, 3, 2 * SP, NZ), BF),
            pltpu.VMEM((2, ROWS, NZ), BF),
            pltpu.VMEM((8, 2 * SP, FINE // 2), BF),
            pltpu.VMEM((8, 2 * SP, FINE // 2), BF),
            pltpu.VMEM((8, 2 * SP, FINE // 2), BF),
            pltpu.VMEM((8, 2 * SP, FINE // 2), BF),
            pltpu.VMEM((6, 6, S, NZ), F32),
            dma((6,)),
            dma((2,)),
            dma((4,)),
            dma((4,)),
            dma((8,)),
            dma((8,)),
            dma((8,)),
            dma((8,)),
            dma((6,)),
        ],
        compiler_params=pltpu.CompilerParams(
            collective_id=0, has_side_effects=True, vmem_limit_bytes=56 * 1024 * 1024
        ),
        name="amr_step",
    )(
        jnp.transpose(coarse_state, (1, 2, 0, 3)),
        jnp.transpose(fine_state, (1, 0, 2)),
        diffusion,
        rate,
        box_pos,
        box_owner,
        *consts,
    )
    return jnp.transpose(coarse, (2, 0, 1, 3)), jnp.transpose(fine, (1, 0, 2))


def solution(mesh):
    in_specs = (
        P(None, "gx", "yz", None),
        P(("gx", "yz"), None, None),
        P(),
        P(),
        P("gx", "yz", None),
        P("gx", "yz", None),
    )
    out_specs = (P(None, "gx", "yz", None), P(("gx", "yz"), None, None))
    consts = [np.asarray(c).astype(jnp.bfloat16) for c in constants()]
    body = functools.partial(local, mesh.shape["gx"], mesh.shape["yz"], consts)
    return jax.shard_map(body, mesh=mesh, in_specs=in_specs, out_specs=out_specs, check_vma=False)
```

```python
import functools

import jax
import jax.numpy as jnp
import numpy as np
from jax import lax
from jax.experimental import pallas as pl
from jax.experimental.pallas import tpu as pltpu
from jax.sharding import PartitionSpec as P

S = 21
BF = jnp.bfloat16
F32 = jnp.float32
SP = 24
ROWS = 6 * SP
NZ = 384
PATCH = 384
FINE = 512
SLOT = 176
FACES = 128
FLAG = 21


def constants():
    def patch(at):
        return at[0] * 64 + at[1] * 8 + at[2]

    faces = []
    for axis in range(3):
        for low, inner in ((0, 1), (5, 4)):
            for a in range(1, 5):
                for b in range(1, 5):
                    at, near = [a, b], [a, b]
                    at.insert(axis, low)
                    near.insert(axis, inner)
                    faces.append((tuple(at), tuple(near), axis))
    number = {at: n for n, (at, _, _) in enumerate(faces)}
    touch = np.zeros((FACES, FINE), np.float32)
    lap = np.zeros((FINE, FINE), np.float32)
    mean = np.zeros((FINE, 128), np.float32)
    put_mean = np.zeros((128, PATCH), np.float32)
    cells = [(x, y, z) for x in range(8) for y in range(8) for z in range(8)]
    for cell, at in enumerate(cells):
        lap[cell, cell] = -6.0
        inner = [c // 2 + 1 for c in at]
        box = (inner[0] - 1) * 16 + (inner[1] - 1) * 4 + inner[2] - 1
        mean[cell, box] = 0.125
        put_mean[box, patch(inner)] = 1.0
        for axis, stride in enumerate((64, 8, 1)):
            for step, edge, ghost in ((-1, 0, 0), (1, 7, 5)):
                if at[axis] == edge:
                    cyc = list(inner)
                    cyc[axis] = ghost
                    touch[number[tuple(cyc)], cell] = 1.0
                else:
                    lap[cell + step * stride, cell] = 1.0
    lap_pool = np.concatenate([lap, 0.25 * touch.T], axis=1)
    ghosts = np.zeros((2 * PATCH, 2 * FACES), np.float32)
    fixes = np.zeros((2 * PATCH, PATCH), np.float32)
    put_face = np.zeros((FACES, PATCH), np.float32)
    sides = np.zeros((256, FACES), np.float32)
    for n, (at, near, axis) in enumerate(faces):
        q = patch(at)
        ghosts[q, n] = 1.0
        ghosts[PATCH + q, FACES + n] = 1.0
        fixes[q, q] = 1.0 - 1.5
        fixes[patch(near), q] = -1.0
        fixes[PATCH + q, q] = -0.5
        put_face[n, q] = 1.0
        if n < 64:
            rest = [at[d] for d in range(3) if d != axis]
            sides[n // 16 * 64 + rest[0] * 8 + rest[1], n] = 1.0
    late = (touch @ mean @ put_mean) - 0.5 * put_face
    late[64:] = 0.0
    return (lap_pool, touch, mean, ghosts, fixes, put_face, put_mean, sides, late)


def iota(shape, dim):
    return lax.broadcasted_iota(jnp.int32, shape, dim)


def dot(a, b):
    return jnp.dot(a, b, preferred_element_type=F32)


def dot_nt(a, b):
    return lax.dot_general(a, b, (((1,), (1,)), ((), ())), preferred_element_type=F32)


def one(mask, kind=BF):
    return jnp.where(mask, 1.0, 0.0).astype(kind)


def split(value):
    high = value.astype(BF)
    return high, (value - high.astype(F32)).astype(BF)


def fold(value):
    half = value.shape[1] // 2
    return jnp.concatenate([value[:, :half], value[:, half:]], axis=0)


def unfold(value):
    value = value.astype(F32)
    return jnp.concatenate([value[:SP], value[SP:]], axis=1)


def kernel(
    n_gx,
    n_yz,
    coarse,
    fine,
    diffusion,
    rate,
    box_pos,
    box_owner,
    lap_pool_in,
    touch_in,
    mean_in,
    ghosts_in,
    fixes_in,
    put_face_in,
    put_mean_in,
    sides_in,
    late_in,
    coarse_out,
    fine_out,
    cv,
    fv,
    lap_pool,
    touch,
    mean,
    ghosts,
    fixes,
    put_face,
    put_mean,
    sides,
    late,
    rz,
    xf,
    xh,
    adv,
    ysend,
    yrecv,
    xrecv,
    ghost_out,
    ghost_in,
    back_out,
    back_in,
    late_out,
    late_got,
    ov,
    load_sem,
    own_sem,
    halo_send,
    halo_recv,
    ghost_send,
    ghost_recv,
    back_send,
    back_recv,
    late_send,
    late_recv,
    out_sem,
    ready,
):
    gx = lax.axis_index("gx")
    me = lax.axis_index("yz")
    right, left = lax.rem(gx + 1, n_gx), lax.rem(gx + n_gx - 1, n_gx)
    up, down = lax.rem(me + 1, n_yz), lax.rem(me + n_yz - 1, n_yz)
    mesh_id = pl.DeviceIdType.MESH

    barrier = pltpu.get_barrier_semaphore()
    for step in range(1, n_yz):
        pl.semaphore_signal(
            barrier, inc=1, device_id=(gx, lax.rem(me + step, n_yz)), device_id_type=mesh_id
        )
    pl.semaphore_signal(barrier, inc=1, device_id=(left, me), device_id_type=mesh_id)

    loads = [
        pltpu.make_async_copy(src, dst, load_sem.at[n])
        for n, (src, dst) in enumerate(
            [
                (coarse, cv),
                (fine, fv),
                (lap_pool_in, lap_pool),
                (touch_in, touch),
                (mean_in, mean),
                (ghosts_in, ghosts),
                (fixes_in, fixes),
                (put_face_in, put_face),
                (put_mean_in, put_mean),
                (sides_in, sides),
                (late_in, late),
            ]
        )
    ]
    for copy in loads:
        copy.start()

    def remote(src, dst, sends, recvs, at, target):
        return pltpu.make_async_remote_copy(
            src_ref=src,
            dst_ref=dst,
            send_sem=sends.at[at],
            recv_sem=recvs.at[at],
            device_id=target,
            device_id_type=mesh_id,
        )

    def exchange(out, got, sends, recvs, n):
        copies = []
        for step in (4, 3, 5, 2, 6, 1, 7):
            other = lax.rem(me + step, n_yz)
            copies.append(remote(out.at[other], got.at[me], sends, recvs, step, (gx, other)))
            copies[-1].start()
        own = pltpu.make_async_copy(out.at[me], got.at[me], own_sem.at[n])
        own.start()
        return copies, own

    loads[0].wait()
    for x in range(6):
        value = jnp.concatenate([cv[x], jnp.zeros((6, SP - S, NZ), F32)], axis=1)
        value = value.reshape(ROWS, NZ)
        xf[x] = value
        xh[x] = value.astype(BF)
        if x % 2:
            before = xf[x - 1]
            first = jnp.concatenate([before[:SP], value[:SP]], axis=0)
            last = jnp.concatenate([before[ROWS - SP :], value[ROWS - SP :]], axis=0)
            ysend[0, x // 2] = first.astype(BF)
            ysend[1, x // 2] = last.astype(BF)

    pl.semaphore_wait(barrier, n_yz)
    pl.semaphore_signal(ready, inc=1, device_id=(right, me), device_id_type=mesh_id)
    to_right = remote(xh.at[5], xrecv.at[0], halo_send, halo_recv, 0, (right, me))
    to_left = remote(xh.at[0], xrecv.at[1], halo_send, halo_recv, 1, (left, me))
    to_down = remote(ysend.at[0], yrecv.at[1], halo_send, halo_recv, 2, (gx, down))
    to_up = remote(ysend.at[1], yrecv.at[0], halo_send, halo_recv, 3, (gx, up))
    to_right.start()
    to_down.start()
    to_up.start()

    rz[...] = jnp.zeros_like(rz)
    rz[0:S, 0:S] = rate[...]
    rate_high, rate_low = split(rz[...])
    tall = one(iota((6, SP, 128), 1) == iota((6, SP, 128), 2), F32)
    tall = tall.reshape(ROWS, 128).astype(BF)
    y_row = iota((6, SP, 1), 0).astype(F32).reshape(ROWS, 1)
    lane = iota((1, ROWS), 1)
    y_col = jnp.zeros((1, ROWS), F32)
    for y in range(1, 6):
        y_col = y_col + jnp.where(lane >= y * SP, 1.0, 0.0)

    def mix(part):
        full = dot_nt(dot(tall, part).astype(BF), tall)
        return jnp.where(y_row == y_col, full, 0.0).astype(BF)

    mix_high, mix_low = mix(rate_high), mix(rate_low)
    at = iota((SP, 1), 0)
    column = jnp.zeros((SP, 1), F32)
    for s in range(S):
        column = jnp.where(at == s, diffusion[s], column)
    d_slab = jnp.concatenate([column] * 6, axis=0)
    d_box = jnp.concatenate([column] * 4, axis=0)

    def start_of(index):
        place = jnp.full(index.shape, box_pos[0, 0, 0] * 6, jnp.int32)
        for i in range(1, 4):
            place = jnp.where(index == i, box_pos[0, 0, i] * 6, place)
        return place

    lane = iota((1, 256), 1)
    want = jnp.where((lane & 7) < 6, start_of(lane >> 6) + (lane & 7), -1)
    take = one(iota((NZ, 256), 0) == want)
    y_lane = (iota((1, 256), 1) >> 3) & 7

    def to_patch(slab):
        cells = dot(slab, take)
        patch = jnp.zeros((SP, 256), F32)
        for y in range(6):
            patch = jnp.where(y_lane == y, cells[y * SP : (y + 1) * SP], patch)
        return patch

    def by_box(parts):
        rows = [
            jnp.concatenate([part[:, i * 64 : (i + 1) * 64] for part in parts], axis=1)
            for i in range(4)
        ]
        return jnp.concatenate(rows, axis=0)

    def for_owner(value, owner):
        total = jnp.zeros((SP, value.shape[1]), F32)
        for i in range(4):
            sent = box_owner[0, 0, i] == owner
            total = total + jnp.where(sent, value[i * SP : (i + 1) * SP], 0.0)
        return total

    olds, news = [], []
    for x in range(6):
        value = xf[x]
        high = xh[x]
        low = (value - high.astype(F32)).astype(BF)
        around = pltpu.roll(value, 1, 1) + pltpu.roll(value, NZ - 1, 1) - 6.0 * value
        if x > 0:
            around = around + xf[x - 1]
        if x < 5:
            around = around + xf[x + 1]
        rest = jnp.zeros((SP, NZ), F32)
        around = around + jnp.concatenate([rest, value[: ROWS - SP]], axis=0)
        around = around + jnp.concatenate([value[SP:], rest], axis=0)
        mixed = dot(mix_high, high) + dot(mix_low, high) + dot(mix_high, low)
        value = value + mixed + d_slab * around
        adv[x] = value
        olds.append(to_patch(high))
        news.append(to_patch(value.astype(BF)))
    patches = jnp.concatenate([by_box(olds), by_box(news)], axis=1).astype(BF)
    for n in (5, 6):
        loads[n].wait()
    sent = dot(patches, ghosts[...])
    flag = jnp.concatenate([one(at == FLAG, F32)] * 4, axis=0)
    sent = sent + flag
    for owner in range(8):
        ghost_out[owner] = fold(for_owner(sent, owner)).astype(BF)
    ghost_copies, own_ghost = exchange(ghost_out, ghost_in, ghost_send, ghost_recv, 0)

    for n in (1, 2, 3, 4):
        loads[n].wait()
    field = fv[...].astype(F32).reshape(S * 8, FINE)
    field = jnp.concatenate([field, jnp.zeros((8, FINE), F32)], axis=0)
    tall = one((iota((SLOT, 128), 0) >> 3) == iota((SLOT, 128), 1))
    slot_same = (iota((SLOT, SLOT), 0) & 7) == (iota((SLOT, SLOT), 1) & 7)

    def slot_rate(part):
        full = dot_nt(dot(tall, part).astype(BF), tall)
        return jnp.where(slot_same, 0.5 * full, 0.0).astype(BF)

    slot_high, slot_low = slot_rate(rate_high), slot_rate(rate_low)
    d_slot = [jnp.full((8, 1), diffusion[s], F32) for s in range(S)]
    d_slot = jnp.concatenate(d_slot + [jnp.zeros((8, 1), F32)], axis=0)
    row = iota((SLOT, 8 * SP), 0)
    inward = one(iota((SLOT, 8 * SP), 1) == (row & 7) * SP + (row >> 3))
    row = iota((8, SP, SLOT), 1) * 8 + iota((8, SP, SLOT), 0)
    outward = (row == iota((8, SP, SLOT), 2)) & (iota((8, SP, SLOT), 1) < S)
    outward = one(outward, F32).reshape(8 * SP, SLOT).astype(BF)
    high = field.astype(BF)
    both = dot(high, lap_pool[...])
    pooled = both[:, FINE:]
    field = (
        field + (2.0 * d_slot) * both[:, :FINE] + (dot(slot_high, high) + dot(slot_low, high))
    )

    for copy in ghost_copies:
        copy.wait_recv()
    own_ghost.wait()
    pl.semaphore_wait(ready, 1)
    to_left.start()

    got = jnp.concatenate([unfold(ghost_in[j]) for j in range(8)], axis=0).astype(BF)
    got = dot(inward, got)
    used = jnp.concatenate([got[S * 8 :, 0:1]] * (SLOT // 8), axis=0) > 0.5
    got = got.astype(BF)
    ghost_old = dot(got[:, :FACES], touch[...])
    ghost_mid = 0.5 * (ghost_old + dot(got[:, FACES:], touch[...]))
    field = field + (2.0 * d_slot) * ghost_old
    high, low = split(field)
    both = dot(high, lap_pool[...]) + dot(low, lap_pool[...])
    pooled = pooled + both[:, FINE:]
    field = (
        field
        + (2.0 * d_slot) * (both[:, :FINE] + ghost_mid)
        + (dot(slot_high, high) + dot(slot_low, high) + dot(slot_high, low))
    )
    back = jnp.concatenate([pooled, dot(field.astype(BF), mean[...])], axis=1)
    back = dot(outward, back.astype(BF))
    for host in range(8):
        back_out[host] = fold(back[host * SP : (host + 1) * SP]).astype(BF)
    back_copies, own_back = exchange(back_out, back_in, back_send, back_recv, 1)

    for n in (7, 8, 9, 10):
        loads[n].wait()
    for copy in (to_down, to_up, to_left, to_right):
        copy.wait_recv()
    layers = [
        xrecv[0],
        xrecv[1],
        jnp.concatenate([yrecv[0, pair] for pair in range(3)], axis=0),
        jnp.concatenate([yrecv[1, pair] for pair in range(3)], axis=0),
    ]
    added = by_box([to_patch(layer) for layer in layers]).astype(BF)
    added = dot(added, sides[...])
    for owner in range(8):
        part = for_owner(added, owner)
        first = jnp.concatenate([part[0:8, :64], part[8:16, :64]], axis=1)
        last = jnp.concatenate([part[16:24, :64], jnp.zeros((8, 64), F32)], axis=1)
        late_out[owner] = jnp.concatenate([first, last], axis=0).astype(BF)
    late_copies, own_late = exchange(late_out, late_got, late_send, late_recv, 2)

    lane = iota((256, 1), 0)
    want = jnp.where((lane & 7) < 6, start_of(lane >> 6) + (lane & 7), -1)
    give = one(iota((256, NZ), 1) == want)
    delta = dot(patches, fixes[...])
    delta = delta + d_box * dot(added.astype(BF), late[...])
    for copy in back_copies:
        copy.wait_recv()
    own_back.wait()
    mine = [unfold(back_in[box_owner[0, 0, i]]) for i in range(4)]
    mine = jnp.concatenate(mine, axis=0).astype(BF)
    delta = d_box * (delta + dot(mine[:, :FACES], put_face[...]))
    delta = delta + dot(mine[:, FACES:], put_mean[...])
    zat = iota((1, NZ), 1)
    inside = jnp.zeros((1, NZ), jnp.int32)
    for i in range(4):
        offset = zat - box_pos[0, 0, i] * 6
        inside = inside + jnp.where((offset >= 1) & (offset <= 4), 1, 0)
    stores = []
    rest = jnp.zeros((ROWS - 2 * SP, NZ), F32)
    for x in range(6):
        part = slice((x % 2) * SP, (x % 2 + 1) * SP)
        before = yrecv[0, x // 2].astype(F32)[part]
        after = yrecv[1, x // 2].astype(F32)[part]
        around = jnp.concatenate([before, rest, after], axis=0)
        if x == 0:
            around = around + xrecv[0].astype(F32)
        if x == 5:
            around = around + xrecv[1].astype(F32)
        part = [delta[i * SP : (i + 1) * SP, x * 64 : (x + 1) * 64] for i in range(4)]
        part = jnp.concatenate(part, axis=1)
        cells = [jnp.where(y_lane == y, part, 0.0) for y in range(6)]
        change = dot(jnp.concatenate(cells, axis=0).astype(BF), give)
        total = adv[x] + d_slab * around + change
        if 1 <= x <= 4:
            middle = jnp.where(inside > 0, change[SP : ROWS - SP], total[SP : ROWS - SP])
            total = jnp.concatenate([total[:SP], middle, total[ROWS - SP :]], axis=0)
        ov[x] = total.reshape(6, SP, NZ)[:, :S]
        stores.append(pltpu.make_async_copy(ov.at[x], coarse_out.at[x], out_sem.at[x]))
        stores[-1].start()

    for copy in late_copies:
        copy.wait_recv()
    own_late.wait()
    parts = []
    for j in range(8):
        value = late_got[j].astype(F32)
        parts += [value[:8, :64], value[:8, 64:], value[8:, :64]]
    got = dot(inward, jnp.concatenate(parts, axis=0).astype(BF)).astype(BF)
    field = field + (d_slot * d_slot) * dot(got, touch[0:64])
    field = jnp.where(used, field, 0.0)
    fine_out[...] = field[: S * 8].reshape(S, 8, FINE).astype(BF)

    for copy in [to_right, to_left, to_down, to_up] + ghost_copies + back_copies + late_copies:
        copy.wait_send()
    for copy in stores:
        copy.wait()


def local(n_gx, n_yz, consts, coarse_state, fine_state, diffusion, rate, box_pos, box_owner):
    hbm = pl.BlockSpec(memory_space=pl.ANY)
    vmem = pl.BlockSpec(memory_space=pltpu.VMEM)
    smem = pl.BlockSpec(memory_space=pltpu.SMEM)
    dma = pltpu.SemaphoreType.DMA
    coarse, fine = pl.pallas_call(
        functools.partial(kernel, n_gx, n_yz),
        out_shape=(
            jax.ShapeDtypeStruct((6, 6, S, NZ), F32),
            jax.ShapeDtypeStruct((S, 8, FINE), BF),
        ),
        in_specs=[hbm, hbm, smem, vmem, smem, smem] + [hbm] * len(consts),
        out_specs=(hbm, vmem),
        scratch_shapes=[
            pltpu.VMEM((6, 6, S, NZ), F32),
            pltpu.VMEM((S, 8, FINE), BF),
            *[pltpu.VMEM(c.shape, BF) for c in consts],
            pltpu.VMEM((128, 128), F32),
            pltpu.VMEM((6, ROWS, NZ), F32),
            pltpu.VMEM((6, ROWS, NZ), BF),
            pltpu.VMEM((6, ROWS, NZ), F32),
            pltpu.VMEM((2, 3, 2 * SP, NZ), BF),
            pltpu.VMEM((2, 3, 2 * SP, NZ), BF),
            pltpu.VMEM((2, ROWS, NZ), BF),
            *[pltpu.VMEM((8, 2 * SP, 128), BF)] * 4,
            *[pltpu.VMEM((8, 16, 128), BF)] * 2,
            pltpu.VMEM((6, 6, S, NZ), F32),
            dma((2 + len(consts),)),
            dma((3,)),
            dma((4,)),
            dma((4,)),
            *[dma((8,))] * 6,
            dma((6,)),
            pltpu.SemaphoreType.REGULAR,
        ],
        compiler_params=pltpu.CompilerParams(
            collective_id=0, has_side_effects=True, vmem_limit_bytes=56 * 1024 * 1024
        ),
        name="amr_step",
    )(
        jnp.transpose(coarse_state, (1, 2, 0, 3)),
        jnp.transpose(fine_state, (1, 0, 2)),
        diffusion,
        rate,
        box_pos,
        box_owner,
        *consts,
    )
    return jnp.transpose(coarse, (2, 0, 1, 3)), jnp.transpose(fine, (1, 0, 2))


def solution(mesh):
    in_specs = (
        P(None, "gx", "yz", None),
        P(("gx", "yz"), None, None),
        P(),
        P(),
        P("gx", "yz", None),
        P("gx", "yz", None),
    )
    out_specs = (P(None, "gx", "yz", None), P(("gx", "yz"), None, None))
    consts = [np.asarray(c).astype(jnp.bfloat16) for c in constants()]
    body = functools.partial(local, mesh.shape["gx"], mesh.shape["yz"], consts)
    return jax.shard_map(body, mesh=mesh, in_specs=in_specs, out_specs=out_specs, check_vma=False)
```

```python
import functools

import jax
import jax.numpy as jnp
import numpy as np
from jax import lax
from jax.experimental import pallas as pl
from jax.experimental.pallas import tpu as pltpu
from jax.sharding import PartitionSpec as P

S = 21
BF = jnp.bfloat16
F32 = jnp.float32
SP = 24
ROWS = 6 * SP
NZ = 384
PATCH = 384
FINE = 512
SLOT = 176
FACES = 128
FLAG = 21


def constants():
    def patch(at):
        return at[0] * 64 + at[1] * 8 + at[2]

    faces = []
    for axis in range(3):
        for low, inner in ((0, 1), (5, 4)):
            for a in range(1, 5):
                for b in range(1, 5):
                    at, near = [a, b], [a, b]
                    at.insert(axis, low)
                    near.insert(axis, inner)
                    faces.append((tuple(at), tuple(near), axis))
    number = {at: n for n, (at, _, _) in enumerate(faces)}
    touch = np.zeros((FACES, FINE), np.float32)
    lap = np.zeros((FINE, FINE), np.float32)
    mean = np.zeros((FINE, 256), np.float32)
    put_mean = np.zeros((256, PATCH), np.float32)
    cells = [(x, y, z) for x in range(8) for y in range(8) for z in range(8)]
    for cell, at in enumerate(cells):
        lap[cell, cell] = -6.0
        inner = [c // 2 + 1 for c in at]
        box = 96 + (inner[0] - 1) * 16 + (inner[1] - 1) * 4 + inner[2] - 1
        mean[cell, box] = 0.125
        put_mean[box, patch(inner)] = 1.0
        for axis, stride in enumerate((64, 8, 1)):
            for step, edge, ghost in ((-1, 0, 0), (1, 7, 5)):
                if at[axis] == edge:
                    cyc = list(inner)
                    cyc[axis] = ghost
                    touch[number[tuple(cyc)], cell] = 1.0
                else:
                    lap[cell + step * stride, cell] = 1.0
    lap_pool = np.concatenate([lap, 0.25 * touch.T], axis=1)
    ghosts = np.zeros((2 * PATCH, 2 * FACES), np.float32)
    fixes = np.zeros((2 * PATCH, PATCH), np.float32)
    put_face = np.zeros((FACES, PATCH), np.float32)
    sides = np.zeros((256, FACES), np.float32)
    for n, (at, near, axis) in enumerate(faces):
        q = patch(at)
        ghosts[q, n] = 1.0
        ghosts[PATCH + q, 96 + n] = 1.0
        fixes[q, q] = 1.0 - 1.5
        fixes[patch(near), q] = -1.0
        fixes[PATCH + q, q] = -0.5
        put_face[n, q] = 1.0
        if n < 64:
            rest = [at[d] for d in range(3) if d != axis]
            sides[n // 16 * 64 + rest[0] * 8 + rest[1], n] = 1.0
    late = (touch @ mean @ put_mean) - 0.5 * put_face
    late[64:] = 0.0
    both = np.zeros((2 * FACES, 2 * FINE), np.float32)
    both[:96, :FINE] = touch[:96]
    both[96:192, FINE:] = touch[:96]
    return (lap_pool, both, mean, ghosts, fixes, put_face, put_mean, sides, late)


def iota(shape, dim):
    return lax.broadcasted_iota(jnp.int32, shape, dim)


def dot(a, b):
    return jnp.dot(a, b, preferred_element_type=F32)


def dot_nt(a, b):
    return lax.dot_general(a, b, (((1,), (1,)), ((), ())), preferred_element_type=F32)


def one(mask, kind=BF):
    return jnp.where(mask, 1.0, 0.0).astype(kind)


def split(value):
    high = value.astype(BF)
    return high, (value - high.astype(F32)).astype(BF)


def fold(value, width):
    tiles = [value[n : n + 8, 128 : 128 + width] for n in range(0, SP, 8)]
    if width == 32:
        tiles = [jnp.concatenate(tiles + [jnp.zeros((8, 32), F32)], axis=1)]
    else:
        tiles = [
            jnp.concatenate(tiles[:2], axis=1),
            jnp.concatenate([tiles[2], jnp.zeros((8, 64), F32)], axis=1),
        ]
    return jnp.concatenate([value[:, :128]] + tiles, axis=0)


def unfold(value, width):
    value = value.astype(F32)
    if width == 32:
        tiles = [value[SP:, n * 32 : (n + 1) * 32] for n in range(3)]
    else:
        tiles = [value[SP : SP + 8, :64], value[SP : SP + 8, 64:], value[SP + 8 :, :64]]
    rest = jnp.concatenate([jnp.concatenate(tiles, axis=0), jnp.zeros((SP, 128 - width), F32)], axis=1)
    return jnp.concatenate([value[:SP], rest], axis=1)


def kernel(
    n_gx,
    n_yz,
    coarse,
    fine,
    diffusion_in,
    rate_in,
    box_pos_in,
    box_owner_in,
    lap_pool_in,
    touch_in,
    mean_in,
    ghosts_in,
    fixes_in,
    sides_in,
    late_in,
    adv_out,
    x_out,
    y_out,
    delta_out,
    field_out,
    back_in,
    late_got,
    diffusion,
    rate,
    box_pos,
    box_owner,
    cv,
    fv,
    lap_pool,
    touch,
    mean,
    ghosts,
    fixes,
    sides,
    late,
    rz,
    xf,
    xh,
    adv,
    ysend,
    yrecv,
    xrecv,
    ghost_out,
    ghost_in,
    back_out,
    late_out,
    delta_tmp,
    field_tmp,
    plane_sem,
    load_sem,
    own_sem,
    halo_send,
    halo_recv,
    ghost_send,
    ghost_recv,
    back_send,
    back_recv,
    late_send,
    late_recv,
    out_sem,
    ready,
):
    gx = lax.axis_index("gx")
    me = lax.axis_index("yz")
    right, left = lax.rem(gx + 1, n_gx), lax.rem(gx + n_gx - 1, n_gx)
    up, down = lax.rem(me + 1, n_yz), lax.rem(me + n_yz - 1, n_yz)
    mesh_id = pl.DeviceIdType.MESH

    barrier = pltpu.get_barrier_semaphore()
    for step in range(1, n_yz):
        pl.semaphore_signal(
            barrier, inc=1, device_id=(gx, lax.rem(me + step, n_yz)), device_id_type=mesh_id
        )
    pl.semaphore_signal(barrier, inc=1, device_id=(left, me), device_id_type=mesh_id)

    planes = [pltpu.make_async_copy(coarse.at[x], cv.at[x], plane_sem.at[x]) for x in range(6)]
    small = [
        (rate_in, rate),
        (diffusion_in, diffusion),
        (box_pos_in, box_pos),
        (box_owner_in, box_owner),
    ]
    small = [pltpu.make_async_copy(p[0], p[1], plane_sem.at[6 + n]) for n, p in enumerate(small)]
    for copy in [planes[5]] + small + planes[:5]:
        copy.start()
    loads = [
        pltpu.make_async_copy(src, dst, load_sem.at[n])
        for n, (src, dst) in enumerate(
            [
                (fine, fv),
                (lap_pool_in, lap_pool),
                (touch_in, touch),
                (mean_in, mean),
                (ghosts_in, ghosts),
                (fixes_in, fixes),
                (sides_in, sides),
                (late_in, late),
            ]
        )
    ]
    for copy in loads:
        copy.start()

    def remote(src, dst, sends, recvs, at, target):
        return pltpu.make_async_remote_copy(
            src_ref=src,
            dst_ref=dst,
            send_sem=sends.at[at],
            recv_sem=recvs.at[at],
            device_id=target,
            device_id_type=mesh_id,
        )

    def exchange(out, got, sends, recvs, n):
        copies = []
        for step in (4, 3, 5, 2, 6, 1, 7):
            other = lax.rem(me + step, n_yz)
            copies.append(remote(out.at[other], got.at[me], sends, recvs, step, (gx, other)))
            copies[-1].start()
        own = pltpu.make_async_copy(out.at[me], got.at[me], own_sem.at[n])
        own.start()
        return copies, own

    def slab(x):
        planes[x].wait()
        value = jnp.concatenate([cv[x], jnp.zeros((6, SP - S, NZ), F32)], axis=1)
        value = value.reshape(ROWS, NZ)
        xf[x] = value
        xh[x] = value.astype(BF)

    to_right = remote(xh.at[5], xrecv.at[0], halo_send, halo_recv, 0, (right, me))
    to_left = remote(xh.at[0], xrecv.at[1], halo_send, halo_recv, 1, (left, me))
    to_down = remote(ysend.at[0], yrecv.at[1], halo_send, halo_recv, 2, (gx, down))
    to_up = remote(ysend.at[1], yrecv.at[0], halo_send, halo_recv, 3, (gx, up))
    slab(5)
    pl.semaphore_wait(barrier, n_yz)
    to_right.start()
    pl.semaphore_signal(ready, inc=1, device_id=(right, me), device_id_type=mesh_id)
    for x in range(5):
        slab(x)
    for pair in range(3):
        for side, part in ((0, slice(0, SP)), (1, slice(ROWS - SP, ROWS))):
            layers = [xf[2 * pair, part], xf[2 * pair + 1, part]]
            ysend[side, pair] = jnp.concatenate(layers, axis=0).astype(BF)
    to_down.start()
    to_up.start()

    @pl.when(gx > 1)
    def _():
        pl.semaphore_wait(ready, 1)
        to_left.start()

    for copy in small:
        copy.wait()
    rz[...] = jnp.zeros_like(rz)
    rz[0:S, 0:S] = rate[...]
    rate_high, rate_low = split(rz[...])
    tall = one(iota((6, SP, 128), 1) == iota((6, SP, 128), 2), F32)
    tall = tall.reshape(ROWS, 128).astype(BF)
    y_row = iota((6, SP, 1), 0).astype(F32).reshape(ROWS, 1)
    lane = iota((1, ROWS), 1)
    y_col = jnp.zeros((1, ROWS), F32)
    for y in range(1, 6):
        y_col = y_col + jnp.where(lane >= y * SP, 1.0, 0.0)

    def mix(part):
        full = dot_nt(dot(tall, part).astype(BF), tall)
        return jnp.where(y_row == y_col, full, 0.0).astype(BF)

    mix_high = mix(rate_high)
    mix_both = jnp.concatenate([mix_high, mix(rate_low)], axis=0)
    at = iota((SP, 1), 0)
    column = jnp.zeros((SP, 1), F32)
    for s in range(S):
        column = jnp.where(at == s, diffusion[s], column)
    d_slab = jnp.concatenate([column] * 6, axis=0)
    d_box = jnp.concatenate([column] * 4, axis=0)

    def start_of(index):
        place = jnp.full(index.shape, box_pos[0, 0, 0] * 6, jnp.int32)
        for i in range(1, 4):
            place = jnp.where(index == i, box_pos[0, 0, i] * 6, place)
        return place

    lane = iota((1, 256), 1)
    want = jnp.where((lane & 7) < 6, start_of(lane >> 6) + (lane & 7), -1)
    take = one(iota((NZ, 256), 0) == want)
    y_lane = (iota((1, 256), 1) >> 3) & 7

    def to_patches(slabs):
        cells = dot(jnp.concatenate(slabs, axis=0), take)
        patches = []
        for n in range(0, ROWS * len(slabs), ROWS):
            patch = jnp.zeros((SP, 256), F32)
            for y in range(6):
                patch = jnp.where(y_lane == y, cells[n + y * SP : n + (y + 1) * SP], patch)
            patches.append(patch)
        return patches

    def by_box(parts):
        rows = [
            jnp.concatenate([part[:, i * 64 : (i + 1) * 64] for part in parts], axis=1)
            for i in range(4)
        ]
        return jnp.concatenate(rows, axis=0)

    def for_owner(value, owner):
        total = jnp.zeros((SP, value.shape[1]), F32)
        for i in range(4):
            sent = box_owner[0, 0, i] == owner
            total = total + jnp.where(sent, value[i * SP : (i + 1) * SP], 0.0)
        return total

    stores = []

    def put(src, dst, n):
        stores.append(pltpu.make_async_copy(src, dst, out_sem.at[n]))
        stores[-1].start()

    news = []
    for x in range(6):
        value = xf[x]
        high = xh[x]
        low = (value - high.astype(F32)).astype(BF)
        around = pltpu.roll(value, 1, 1) + pltpu.roll(value, NZ - 1, 1) - 6.0 * value
        if x > 0:
            around = around + xf[x - 1]
        if x < 5:
            around = around + xf[x + 1]
        rest = jnp.zeros((SP, NZ), F32)
        around = around + jnp.concatenate([rest, value[: ROWS - SP]], axis=0)
        around = around + jnp.concatenate([value[SP:], rest], axis=0)
        mixed = dot(mix_both, high)
        mixed = mixed[:ROWS] + mixed[ROWS:] + dot(mix_high, low)
        value = value + mixed + d_slab * around
        adv[x] = value
        put(adv.at[x], adv_out.at[x], x)
        news.append(value.astype(BF))
    olds = by_box(to_patches([xh[x] for x in range(6)]))
    patches = jnp.concatenate([olds, by_box(to_patches(news))], axis=1).astype(BF)
    for n in (4, 5):
        loads[n].wait()
    sent = dot(patches, ghosts[...])
    flag = jnp.concatenate([one(at == FLAG, F32)] * 4, axis=0)
    sent = sent + flag
    for owner in range(8):
        ghost_out[owner] = fold(for_owner(sent, owner), 64).astype(BF)
    ghost_copies, own_ghost = exchange(ghost_out, ghost_in, ghost_send, ghost_recv, 0)

    for n in (0, 1, 2, 3):
        loads[n].wait()
    field = fv[...].astype(F32).reshape(S * 8, FINE)
    field = jnp.concatenate([field, jnp.zeros((8, FINE), F32)], axis=0)
    tall = one((iota((SLOT, 128), 0) >> 3) == iota((SLOT, 128), 1))
    slot_same = (iota((SLOT, SLOT), 0) & 7) == (iota((SLOT, SLOT), 1) & 7)

    def slot_rate(part):
        full = dot_nt(dot(tall, part).astype(BF), tall)
        return jnp.where(slot_same, 0.5 * full, 0.0).astype(BF)

    slot_high = slot_rate(rate_high)
    slot_both = jnp.concatenate([slot_high, slot_rate(rate_low)], axis=0)
    d_slot = [jnp.full((8, 1), diffusion[s], F32) for s in range(S)]
    d_slot = jnp.concatenate(d_slot + [jnp.zeros((8, 1), F32)], axis=0)
    row = iota((SLOT, 8 * SP), 0)
    inward = one(iota((SLOT, 8 * SP), 1) == (row & 7) * SP + (row >> 3))
    row = iota((8, SP, SLOT), 1) * 8 + iota((8, SP, SLOT), 0)
    outward = (row == iota((8, SP, SLOT), 2)) & (iota((8, SP, SLOT), 1) < S)
    outward = one(outward, F32).reshape(8 * SP, SLOT).astype(BF)
    high = field.astype(BF)
    both = dot(high, lap_pool[...])
    mixed = dot(slot_both, high)
    pooled = both[:, FINE:]
    field = (
        field + (2.0 * d_slot) * both[:, :FINE] + mixed[:SLOT] + mixed[SLOT:]
    )

    for copy in ghost_copies:
        copy.wait_recv()
    own_ghost.wait()

    got = jnp.concatenate([unfold(ghost_in[j], 64) for j in range(8)], axis=0).astype(BF)
    got = dot(inward, got)
    used = jnp.concatenate([got[S * 8 :, 0:1]] * (SLOT // 8), axis=0) > 0.5
    got = got.astype(BF)
    spread = dot(got, touch[...])
    ghost_old = spread[:, :FINE]
    ghost_mid = 0.5 * (ghost_old + spread[:, FINE:])
    field = field + (2.0 * d_slot) * ghost_old
    high, low = split(field)
    both = dot(jnp.concatenate([high, low], axis=0), lap_pool[...])
    both = both[:SLOT] + both[SLOT:]
    mixed = dot(slot_both, high)
    pooled = pooled + both[:, FINE:]
    field = (
        field
        + (2.0 * d_slot) * (both[:, :FINE] + ghost_mid)
        + (mixed[:SLOT] + mixed[SLOT:] + dot(slot_high, low))
    )
    field_tmp[...] = jnp.where(used, field, 0.0)
    back = dot(field.astype(BF), mean[...])
    back = jnp.concatenate([back[:, :FACES] + pooled, back[:, FACES:]], axis=1)
    back = dot(outward, back.astype(BF))
    for host in range(8):
        back_out[host] = fold(back[host * SP : (host + 1) * SP], 32).astype(BF)
    back_copies, own_back = exchange(back_out, back_in, back_send, back_recv, 1)

    put(field_tmp, field_out, 6)

    @pl.when(gx <= 1)
    def _():
        pl.semaphore_wait(ready, 1)
        to_left.start()

    for n in (6, 7):
        loads[n].wait()
    delta = dot(patches, fixes[...])
    to_down.wait_recv()
    to_up.wait_recv()
    put(yrecv, y_out, 7)
    layers = [jnp.concatenate([yrecv[n, pair] for pair in range(3)], axis=0) for n in range(2)]
    to_left.wait_recv()
    put(xrecv.at[1], x_out.at[1], 8)
    parts = to_patches([xrecv[1]] + layers)
    to_right.wait_recv()
    put(xrecv.at[0], x_out.at[0], 9)
    parts = to_patches([xrecv[0]]) + parts
    added = by_box(parts).astype(BF)
    added = dot(added, sides[...])
    for owner in range(8):
        part = for_owner(added, owner)
        first = jnp.concatenate([part[0:8, :64], part[8:16, :64]], axis=1)
        last = jnp.concatenate([part[16:24, :64], jnp.zeros((8, 64), F32)], axis=1)
        late_out[owner] = jnp.concatenate([first, last], axis=0).astype(BF)
    late_copies, own_late = exchange(late_out, late_got, late_send, late_recv, 2)

    delta_tmp[...] = d_box * (delta + d_box * dot(added.astype(BF), late[...]))
    put(delta_tmp, delta_out, 10)

    for copy in [to_right, to_left, to_down, to_up] + ghost_copies:
        copy.wait_send()
    for copy in back_copies + late_copies:
        copy.wait()
    own_back.wait()
    own_late.wait()
    for copy in stores:
        copy.wait()


def finish(
    adv_in,
    x_in,
    y_in,
    delta_in,
    field_in,
    back_in,
    late_in,
    touch_in,
    put_face_in,
    put_mean_in,
    diffusion_in,
    box_pos_in,
    box_owner_in,
    coarse_out,
    fine_out,
    diffusion,
    box_pos,
    box_owner,
    adv,
    x_halo,
    y_halo,
    delta_part,
    field,
    back,
    late_got,
    touch,
    put_face,
    put_mean,
    ov,
    fv,
    load_sem,
    out_sem,
):
    pairs = [
        (back_in, back),
        (put_face_in, put_face),
        (put_mean_in, put_mean),
        (delta_in, delta_part),
        (x_in, x_halo),
        (y_in, y_halo),
        (late_in, late_got),
        (touch_in, touch),
        (field_in, field),
    ]
    pairs += [(adv_in.at[x], adv.at[x]) for x in range(6)]
    loads = [pltpu.make_async_copy(p[0], p[1], load_sem.at[n]) for n, p in enumerate(pairs)]
    small = [(box_pos_in, box_pos), (box_owner_in, box_owner), (diffusion_in, diffusion)]
    small = [pltpu.make_async_copy(p[0], p[1], load_sem.at[15 + n]) for n, p in enumerate(small)]
    for copy in small + loads:
        copy.start()
    for copy in small:
        copy.wait()

    at = iota((SP, 1), 0)
    column = jnp.zeros((SP, 1), F32)
    for s in range(S):
        column = jnp.where(at == s, diffusion[s], column)
    d_slab = jnp.concatenate([column] * 6, axis=0)
    d_box = jnp.concatenate([column] * 4, axis=0)
    d_slot = [jnp.full((8, 1), diffusion[s], F32) for s in range(S)]
    d_slot = jnp.concatenate(d_slot + [jnp.zeros((8, 1), F32)], axis=0)
    row = iota((SLOT, 8 * SP), 0)
    inward = one(iota((SLOT, 8 * SP), 1) == (row & 7) * SP + (row >> 3))
    lane = iota((256, 1), 0)
    place = jnp.full((256, 1), box_pos[0, 0, 0] * 6, jnp.int32)
    for i in range(1, 4):
        place = jnp.where((lane >> 6) == i, box_pos[0, 0, i] * 6, place)
    give = one(iota((256, NZ), 1) == jnp.where((lane & 7) < 6, place + (lane & 7), -1))
    y_lane = (iota((1, 256), 1) >> 3) & 7
    zat = iota((1, NZ), 1)
    inside = jnp.zeros((1, NZ), jnp.int32)
    for i in range(4):
        offset = zat - box_pos[0, 0, i] * 6
        inside = inside + jnp.where((offset >= 1) & (offset <= 4), 1, 0)

    for copy in loads[:4]:
        copy.wait()
    mine = [unfold(back[box_owner[0, 0, i]], 32) for i in range(4)]
    mine = jnp.concatenate(mine, axis=0).astype(BF)
    delta = delta_part[...] + d_box * dot(mine[:, :FACES], put_face[...])
    delta = delta + dot(mine, put_mean[...])
    cells = []
    for x in range(6):
        part = [delta[i * SP : (i + 1) * SP, x * 64 : (x + 1) * 64] for i in range(4)]
        part = jnp.concatenate(part, axis=1)
        cells += [jnp.where(y_lane == y, part, 0.0) for y in range(6)]
    changes = dot(jnp.concatenate(cells, axis=0).astype(BF), give)
    for copy in loads[4:6]:
        copy.wait()
    stores = []
    rest = jnp.zeros((ROWS - 2 * SP, NZ), F32)
    for x in range(6):
        loads[9 + x].wait()
        part = slice((x % 2) * SP, (x % 2 + 1) * SP)
        before = y_halo[0, x // 2].astype(F32)[part]
        after = y_halo[1, x // 2].astype(F32)[part]
        around = jnp.concatenate([before, rest, after], axis=0)
        if x == 0:
            around = around + x_halo[0].astype(F32)
        if x == 5:
            around = around + x_halo[1].astype(F32)
        change = changes[x * ROWS : (x + 1) * ROWS]
        total = adv[x] + d_slab * around + change
        if 1 <= x <= 4:
            middle = jnp.where(inside > 0, change[SP : ROWS - SP], total[SP : ROWS - SP])
            total = jnp.concatenate([total[:SP], middle, total[ROWS - SP :]], axis=0)
        ov[x] = total.reshape(6, SP, NZ)[:, :S]
        stores.append(pltpu.make_async_copy(ov.at[x], coarse_out.at[x], out_sem.at[x]))
        stores[-1].start()

    for copy in loads[6:9]:
        copy.wait()
    parts = []
    for j in range(8):
        value = late_got[j].astype(F32)
        parts += [value[:8, :64], value[:8, 64:], value[8:, :64]]
    got = dot(inward, jnp.concatenate(parts, axis=0).astype(BF)).astype(BF)
    total = field[...] + (d_slot * d_slot) * dot(got, touch[...])
    fv[...] = total[: S * 8].reshape(S, 8, FINE).astype(BF)
    stores.append(pltpu.make_async_copy(fv, fine_out, out_sem.at[6]))
    stores[-1].start()
    for copy in stores:
        copy.wait()


def local(n_gx, n_yz, consts, coarse_state, fine_state, diffusion, rate, box_pos, box_owner):
    hbm = pl.BlockSpec(memory_space=pl.ANY)
    dma = pltpu.SemaphoreType.DMA
    first = [consts[n] for n in (0, 1, 2, 3, 4, 7, 8)]
    middle = [
        ((6, ROWS, NZ), F32),
        ((2, ROWS, NZ), BF),
        ((2, 3, 2 * SP, NZ), BF),
        ((4 * SP, PATCH), F32),
        ((SLOT, FINE), F32),
        ((8, 32, 128), BF),
        ((8, 16, 128), BF),
    ]
    between = pl.pallas_call(
        functools.partial(kernel, n_gx, n_yz),
        out_shape=tuple(jax.ShapeDtypeStruct(*m) for m in middle),
        in_specs=[hbm] * (6 + len(first)),
        out_specs=(hbm,) * len(middle),
        scratch_shapes=[
            pltpu.SMEM((S,), F32),
            pltpu.VMEM((S, S), F32),
            pltpu.SMEM((1, 1, 4), jnp.int32),
            pltpu.SMEM((1, 1, 4), jnp.int32),
            pltpu.VMEM((6, 6, S, NZ), F32),
            pltpu.VMEM((S, 8, FINE), BF),
            *[pltpu.VMEM(c.shape, BF) for c in first],
            pltpu.VMEM((128, 128), F32),
            pltpu.VMEM((6, ROWS, NZ), F32),
            pltpu.VMEM((6, ROWS, NZ), BF),
            pltpu.VMEM((6, ROWS, NZ), F32),
            pltpu.VMEM((2, 3, 2 * SP, NZ), BF),
            pltpu.VMEM((2, 3, 2 * SP, NZ), BF),
            pltpu.VMEM((2, ROWS, NZ), BF),
            *[pltpu.VMEM((8, 40, 128), BF)] * 2,
            pltpu.VMEM((8, 32, 128), BF),
            pltpu.VMEM((8, 16, 128), BF),
            pltpu.VMEM((4 * SP, PATCH), F32),
            pltpu.VMEM((SLOT, FINE), F32),
            dma((10,)),
            dma((1 + len(first),)),
            dma((3,)),
            dma((4,)),
            dma((4,)),
            *[dma((8,))] * 6,
            dma((11,)),
            pltpu.SemaphoreType.REGULAR,
        ],
        compiler_params=pltpu.CompilerParams(
            collective_id=0, has_side_effects=True, vmem_limit_bytes=56 * 1024 * 1024
        ),
        name="amr_step",
    )(
        jnp.transpose(coarse_state, (1, 2, 0, 3)),
        jnp.transpose(fine_state, (1, 0, 2)),
        diffusion,
        rate,
        box_pos,
        box_owner,
        *first,
    )
    last = [consts[1][:64, :FINE], consts[5], consts[6]]
    coarse, fine = pl.pallas_call(
        finish,
        out_shape=(
            jax.ShapeDtypeStruct((6, 6, S, NZ), F32),
            jax.ShapeDtypeStruct((S, 8, FINE), BF),
        ),
        in_specs=[hbm] * (len(middle) + len(last) + 3),
        out_specs=(hbm, hbm),
        scratch_shapes=[
            pltpu.SMEM((S,), F32),
            pltpu.SMEM((1, 1, 4), jnp.int32),
            pltpu.SMEM((1, 1, 4), jnp.int32),
            *[pltpu.VMEM(*m) for m in middle],
            *[pltpu.VMEM(c.shape, BF) for c in last],
            pltpu.VMEM((6, 6, S, NZ), F32),
            pltpu.VMEM((S, 8, FINE), BF),
            dma((18,)),
            dma((7,)),
        ],
        compiler_params=pltpu.CompilerParams(vmem_limit_bytes=56 * 1024 * 1024),
        name="finish",
    )(*between, *last, diffusion, box_pos, box_owner)
    return jnp.transpose(coarse, (2, 0, 1, 3)), jnp.transpose(fine, (1, 0, 2))


def solution(mesh):
    in_specs = (
        P(None, "gx", "yz", None),
        P(("gx", "yz"), None, None),
        P(),
        P(),
        P("gx", "yz", None),
        P("gx", "yz", None),
    )
    out_specs = (P(None, "gx", "yz", None), P(("gx", "yz"), None, None))
    consts = [np.asarray(c).astype(jnp.bfloat16) for c in constants()]
    body = functools.partial(local, mesh.shape["gx"], mesh.shape["yz"], consts)
    return jax.shard_map(body, mesh=mesh, in_specs=in_specs, out_specs=out_specs, check_vma=False)
```

```python
import functools

import jax
import jax.numpy as jnp
import numpy as np
from jax import lax
from jax.experimental import pallas as pl
from jax.experimental.pallas import tpu as pltpu
from jax.sharding import PartitionSpec as P

S = 21
BF = jnp.bfloat16
F32 = jnp.float32
SP = 24
ROWS = 6 * SP
NZ = 384
PATCH = 384
FINE = 512
SLOT = 176
FACES = 128
FLAG = 21


def constants():
    def patch(at):
        return at[0] * 64 + at[1] * 8 + at[2]

    faces = []
    for axis in range(3):
        for low, inner in ((0, 1), (5, 4)):
            for a in range(1, 5):
                for b in range(1, 5):
                    at, near = [a, b], [a, b]
                    at.insert(axis, low)
                    near.insert(axis, inner)
                    faces.append((tuple(at), tuple(near), axis))
    number = {at: n for n, (at, _, _) in enumerate(faces)}
    touch = np.zeros((FACES, FINE), np.float32)
    lap = np.zeros((FINE, FINE), np.float32)
    mean = np.zeros((FINE, 256), np.float32)
    put_mean = np.zeros((256, PATCH), np.float32)
    cells = [(x, y, z) for x in range(8) for y in range(8) for z in range(8)]
    for cell, at in enumerate(cells):
        lap[cell, cell] = -6.0
        inner = [c // 2 + 1 for c in at]
        box = 96 + (inner[0] - 1) * 16 + (inner[1] - 1) * 4 + inner[2] - 1
        mean[cell, box] = 0.125
        put_mean[box, patch(inner)] = 1.0
        for axis, stride in enumerate((64, 8, 1)):
            for step, edge, ghost in ((-1, 0, 0), (1, 7, 5)):
                if at[axis] == edge:
                    cyc = list(inner)
                    cyc[axis] = ghost
                    touch[number[tuple(cyc)], cell] = 1.0
                else:
                    lap[cell + step * stride, cell] = 1.0
    lap_pool = np.concatenate([lap, 0.25 * touch.T], axis=1)
    ghosts = np.zeros((2 * PATCH, 2 * FACES), np.float32)
    fixes = np.zeros((2 * PATCH, PATCH), np.float32)
    put_face = np.zeros((FACES, PATCH), np.float32)
    sides = np.zeros((256, FACES), np.float32)
    for n, (at, near, axis) in enumerate(faces):
        q = patch(at)
        ghosts[q, n] = 1.0
        ghosts[PATCH + q, 96 + n] = 1.0
        fixes[q, q] = 1.0 - 1.5
        fixes[patch(near), q] = -1.0
        fixes[PATCH + q, q] = -0.5
        put_face[n, q] = 1.0
        if n < 64:
            rest = [at[d] for d in range(3) if d != axis]
            sides[n // 16 * 64 + rest[0] * 8 + rest[1], n] = 1.0
    late = (touch @ mean @ put_mean) - 0.5 * put_face
    late[64:] = 0.0
    both = np.zeros((2 * FACES, 2 * FINE), np.float32)
    both[:96, :FINE] = touch[:96]
    both[96:192, FINE:] = touch[:96]
    return (lap_pool, both, mean, ghosts, fixes, put_face, put_mean, sides, late)


def iota(shape, dim):
    return lax.broadcasted_iota(jnp.int32, shape, dim)


def dot(a, b):
    return jnp.dot(a, b, preferred_element_type=F32)


def dot_nt(a, b):
    return lax.dot_general(a, b, (((1,), (1,)), ((), ())), preferred_element_type=F32)


def one(mask, kind=BF):
    return jnp.where(mask, 1.0, 0.0).astype(kind)


def split(value):
    high = value.astype(BF)
    return high, (value - high.astype(F32)).astype(BF)


def fold(value, width):
    tiles = [value[n : n + 8, 128 : 128 + width] for n in range(0, SP, 8)]
    if width == 32:
        tiles = [jnp.concatenate(tiles + [jnp.zeros((8, 32), F32)], axis=1)]
    else:
        tiles = [
            jnp.concatenate(tiles[:2], axis=1),
            jnp.concatenate([tiles[2], jnp.zeros((8, 64), F32)], axis=1),
        ]
    return jnp.concatenate([value[:, :128]] + tiles, axis=0)


def unfold(value, width):
    value = value.astype(F32)
    if width == 32:
        tiles = [value[SP:, n * 32 : (n + 1) * 32] for n in range(3)]
    else:
        tiles = [value[SP : SP + 8, :64], value[SP : SP + 8, 64:], value[SP + 8 :, :64]]
    rest = jnp.concatenate([jnp.concatenate(tiles, axis=0), jnp.zeros((SP, 128 - width), F32)], axis=1)
    return jnp.concatenate([value[:SP], rest], axis=1)


def kernel(
    n_gx,
    n_yz,
    coarse,
    fine,
    diffusion_in,
    rate_in,
    box_pos_in,
    box_owner_in,
    lap_pool_in,
    touch_in,
    mean_in,
    ghosts_in,
    fixes_in,
    put_face_in,
    put_mean_in,
    sides_in,
    late_in,
    coarse_mid,
    field_out,
    late_got,
    diffusion,
    rate,
    box_pos,
    box_owner,
    cv,
    fv,
    lap_pool,
    touch,
    mean,
    ghosts,
    fixes,
    put_face,
    put_mean,
    sides,
    late,
    rz,
    xf,
    xh,
    adv,
    ysend,
    yrecv,
    xrecv,
    ghost_out,
    ghost_in,
    back_out,
    back_in,
    late_out,
    field_tmp,
    ov,
    plane_sem,
    load_sem,
    own_sem,
    halo_send,
    halo_recv,
    ghost_send,
    ghost_recv,
    back_send,
    back_recv,
    late_send,
    late_recv,
    out_sem,
    ready,
):
    gx = lax.axis_index("gx")
    me = lax.axis_index("yz")
    right, left = lax.rem(gx + 1, n_gx), lax.rem(gx + n_gx - 1, n_gx)
    up, down = lax.rem(me + 1, n_yz), lax.rem(me + n_yz - 1, n_yz)
    mesh_id = pl.DeviceIdType.MESH

    planes = [pltpu.make_async_copy(coarse.at[x], cv.at[x], plane_sem.at[x]) for x in range(6)]
    planes[5].start()

    barrier = pltpu.get_barrier_semaphore()
    for step in range(1, n_yz):
        pl.semaphore_signal(
            barrier, inc=1, device_id=(gx, lax.rem(me + step, n_yz)), device_id_type=mesh_id
        )
    pl.semaphore_signal(barrier, inc=1, device_id=(left, me), device_id_type=mesh_id)

    small = [
        (rate_in, rate),
        (diffusion_in, diffusion),
        (box_pos_in, box_pos),
        (box_owner_in, box_owner),
    ]
    small = [pltpu.make_async_copy(p[0], p[1], plane_sem.at[6 + n]) for n, p in enumerate(small)]
    for copy in small + planes[:5]:
        copy.start()
    loads = [
        pltpu.make_async_copy(src, dst, load_sem.at[n])
        for n, (src, dst) in enumerate(
            [
                (fine, fv),
                (lap_pool_in, lap_pool),
                (touch_in, touch),
                (mean_in, mean),
                (ghosts_in, ghosts),
                (fixes_in, fixes),
                (put_face_in, put_face),
                (put_mean_in, put_mean),
                (sides_in, sides),
                (late_in, late),
            ]
        )
    ]
    for copy in loads:
        copy.start()

    def remote(src, dst, sends, recvs, at, target):
        return pltpu.make_async_remote_copy(
            src_ref=src,
            dst_ref=dst,
            send_sem=sends.at[at],
            recv_sem=recvs.at[at],
            device_id=target,
            device_id_type=mesh_id,
        )

    def exchange(out, got, sends, recvs, n):
        copies = []
        for step in (4, 3, 5, 2, 6, 1, 7):
            other = lax.rem(me + step, n_yz)
            copies.append(remote(out.at[other], got.at[me], sends, recvs, step, (gx, other)))
            copies[-1].start()
        own = pltpu.make_async_copy(out.at[me], got.at[me], own_sem.at[n])
        own.start()
        return copies, own

    def slab(x):
        planes[x].wait()
        value = jnp.concatenate([cv[x], jnp.zeros((6, SP - S, NZ), F32)], axis=1)
        value = value.reshape(ROWS, NZ)
        xf[x] = value
        xh[x] = value.astype(BF)

    to_right = remote(xh.at[5], xrecv.at[0], halo_send, halo_recv, 0, (right, me))
    to_left = remote(xh.at[0], xrecv.at[1], halo_send, halo_recv, 1, (left, me))
    to_down = remote(ysend.at[0], yrecv.at[1], halo_send, halo_recv, 2, (gx, down))
    to_up = remote(ysend.at[1], yrecv.at[0], halo_send, halo_recv, 3, (gx, up))
    slab(5)
    pl.semaphore_wait(barrier, n_yz)
    to_right.start()
    pl.semaphore_signal(ready, inc=1, device_id=(right, me), device_id_type=mesh_id)
    for x in range(5):
        slab(x)
    for pair in range(3):
        for side, part in ((0, slice(0, SP)), (1, slice(ROWS - SP, ROWS))):
            layers = [xf[2 * pair, part], xf[2 * pair + 1, part]]
            ysend[side, pair] = jnp.concatenate(layers, axis=0).astype(BF)
    to_down.start()
    to_up.start()

    @pl.when(gx > 1)
    def _():
        pl.semaphore_wait(ready, 1)
        to_left.start()

    for copy in small:
        copy.wait()
    rz[...] = jnp.zeros_like(rz)
    rz[0:S, 0:S] = rate[...]
    rate_high, rate_low = split(rz[...])
    tall = one(iota((6, SP, 128), 1) == iota((6, SP, 128), 2), F32)
    tall = tall.reshape(ROWS, 128).astype(BF)
    y_row = iota((6, SP, 1), 0).astype(F32).reshape(ROWS, 1)
    lane = iota((1, ROWS), 1)
    y_col = jnp.zeros((1, ROWS), F32)
    for y in range(1, 6):
        y_col = y_col + jnp.where(lane >= y * SP, 1.0, 0.0)

    def mix(part):
        full = dot_nt(dot(tall, part).astype(BF), tall)
        return jnp.where(y_row == y_col, full, 0.0).astype(BF)

    mix_high = mix(rate_high)
    mix_both = jnp.concatenate([mix_high, mix(rate_low)], axis=0)
    at = iota((SP, 1), 0)
    column = jnp.zeros((SP, 1), F32)
    for s in range(S):
        column = jnp.where(at == s, diffusion[s], column)
    d_slab = jnp.concatenate([column] * 6, axis=0)
    d_box = jnp.concatenate([column] * 4, axis=0)

    def start_of(index):
        place = jnp.full(index.shape, box_pos[0, 0, 0] * 6, jnp.int32)
        for i in range(1, 4):
            place = jnp.where(index == i, box_pos[0, 0, i] * 6, place)
        return place

    lane = iota((1, 256), 1)
    want = jnp.where((lane & 7) < 6, start_of(lane >> 6) + (lane & 7), -1)
    take = one(iota((NZ, 256), 0) == want)
    y_lane = (iota((1, 256), 1) >> 3) & 7

    def to_patches(slabs):
        cells = dot(jnp.concatenate(slabs, axis=0), take)
        patches = []
        for n in range(0, ROWS * len(slabs), ROWS):
            patch = jnp.zeros((SP, 256), F32)
            for y in range(6):
                patch = jnp.where(y_lane == y, cells[n + y * SP : n + (y + 1) * SP], patch)
            patches.append(patch)
        return patches

    def by_box(parts):
        rows = [
            jnp.concatenate([part[:, i * 64 : (i + 1) * 64] for part in parts], axis=1)
            for i in range(4)
        ]
        return jnp.concatenate(rows, axis=0)

    def for_owner(value, owner):
        total = jnp.zeros((SP, value.shape[1]), F32)
        for i in range(4):
            sent = box_owner[0, 0, i] == owner
            total = total + jnp.where(sent, value[i * SP : (i + 1) * SP], 0.0)
        return total

    stores = []

    def put(src, dst, n):
        stores.append(pltpu.make_async_copy(src, dst, out_sem.at[n]))
        stores[-1].start()

    news = []
    for x in range(6):
        value = xf[x]
        high = xh[x]
        low = (value - high.astype(F32)).astype(BF)
        around = pltpu.roll(value, 1, 1) + pltpu.roll(value, NZ - 1, 1) - 6.0 * value
        if x > 0:
            around = around + xf[x - 1]
        if x < 5:
            around = around + xf[x + 1]
        rest = jnp.zeros((SP, NZ), F32)
        around = around + jnp.concatenate([rest, value[: ROWS - SP]], axis=0)
        around = around + jnp.concatenate([value[SP:], rest], axis=0)
        mixed = dot(mix_both, high)
        mixed = mixed[:ROWS] + mixed[ROWS:] + dot(mix_high, low)
        value = value + mixed + d_slab * around
        adv[x] = value
        news.append(value.astype(BF))
    olds = by_box(to_patches([xh[x] for x in range(6)]))
    patches = jnp.concatenate([olds, by_box(to_patches(news))], axis=1).astype(BF)
    for n in (4, 5):
        loads[n].wait()
    sent = dot(patches, ghosts[...])
    flag = jnp.concatenate([one(at == FLAG, F32)] * 4, axis=0)
    sent = sent + flag
    for owner in range(8):
        ghost_out[owner] = fold(for_owner(sent, owner), 64).astype(BF)
    ghost_copies, own_ghost = exchange(ghost_out, ghost_in, ghost_send, ghost_recv, 0)

    for n in (0, 1, 2, 3):
        loads[n].wait()
    field = fv[...].astype(F32).reshape(S * 8, FINE)
    field = jnp.concatenate([field, jnp.zeros((8, FINE), F32)], axis=0)
    tall = one((iota((SLOT, 128), 0) >> 3) == iota((SLOT, 128), 1))
    slot_same = (iota((SLOT, SLOT), 0) & 7) == (iota((SLOT, SLOT), 1) & 7)

    def slot_rate(part):
        full = dot_nt(dot(tall, part).astype(BF), tall)
        return jnp.where(slot_same, 0.5 * full, 0.0).astype(BF)

    slot_high = slot_rate(rate_high)
    slot_both = jnp.concatenate([slot_high, slot_rate(rate_low)], axis=0)
    d_slot = [jnp.full((8, 1), diffusion[s], F32) for s in range(S)]
    d_slot = jnp.concatenate(d_slot + [jnp.zeros((8, 1), F32)], axis=0)
    row = iota((SLOT, 8 * SP), 0)
    inward = one(iota((SLOT, 8 * SP), 1) == (row & 7) * SP + (row >> 3))
    row = iota((8, SP, SLOT), 1) * 8 + iota((8, SP, SLOT), 0)
    outward = (row == iota((8, SP, SLOT), 2)) & (iota((8, SP, SLOT), 1) < S)
    outward = one(outward, F32).reshape(8 * SP, SLOT).astype(BF)
    high = field.astype(BF)
    both = dot(high, lap_pool[...])
    mixed = dot(slot_both, high)
    pooled = both[:, FINE:]
    field = (
        field + (2.0 * d_slot) * both[:, :FINE] + mixed[:SLOT] + mixed[SLOT:]
    )

    for copy in ghost_copies:
        copy.wait_recv()
    own_ghost.wait()

    got = jnp.concatenate([unfold(ghost_in[j], 64) for j in range(8)], axis=0).astype(BF)
    got = dot(inward, got)
    used = jnp.concatenate([got[S * 8 :, 0:1]] * (SLOT // 8), axis=0) > 0.5
    got = got.astype(BF)
    spread = dot(got, touch[...])
    ghost_old = spread[:, :FINE]
    ghost_mid = 0.5 * (ghost_old + spread[:, FINE:])
    field = field + (2.0 * d_slot) * ghost_old
    high, low = split(field)
    both = dot(jnp.concatenate([high, low], axis=0), lap_pool[...])
    both = both[:SLOT] + both[SLOT:]
    mixed = dot(slot_both, high)
    pooled = pooled + both[:, FINE:]
    field = (
        field
        + (2.0 * d_slot) * (both[:, :FINE] + ghost_mid)
        + (mixed[:SLOT] + mixed[SLOT:] + dot(slot_high, low))
    )
    field_tmp[...] = jnp.where(used, field, 0.0)
    back = dot(field.astype(BF), mean[...])
    back = jnp.concatenate([back[:, :FACES] + pooled, back[:, FACES:]], axis=1)
    back = dot(outward, back.astype(BF))
    for host in range(8):
        back_out[host] = fold(back[host * SP : (host + 1) * SP], 32).astype(BF)
    back_copies, own_back = exchange(back_out, back_in, back_send, back_recv, 1)

    put(field_tmp, field_out, 6)

    lane = iota((256, 1), 0)
    want = jnp.where((lane & 7) < 6, start_of(lane >> 6) + (lane & 7), -1)
    give = one(iota((256, NZ), 1) == want)
    zat = iota((1, NZ), 1)
    inside = jnp.zeros((1, NZ), jnp.int32)
    for i in range(4):
        offset = zat - box_pos[0, 0, i] * 6
        inside = inside + jnp.where((offset >= 1) & (offset <= 4), 1, 0)

    @pl.when(gx <= 1)
    def _():
        pl.semaphore_wait(ready, 1)
        to_left.start()

    for n in (6, 7, 8, 9):
        loads[n].wait()
    delta = dot(patches, fixes[...])
    to_down.wait_recv()
    to_up.wait_recv()
    layers = [jnp.concatenate([yrecv[n, pair] for pair in range(3)], axis=0) for n in range(2)]
    to_left.wait_recv()
    parts = to_patches([xrecv[1]] + layers)
    to_right.wait_recv()
    parts = to_patches([xrecv[0]]) + parts
    added = by_box(parts).astype(BF)
    added = dot(added, sides[...])
    for owner in range(8):
        part = for_owner(added, owner)
        first = jnp.concatenate([part[0:8, :64], part[8:16, :64]], axis=1)
        last = jnp.concatenate([part[16:24, :64], jnp.zeros((8, 64), F32)], axis=1)
        late_out[owner] = jnp.concatenate([first, last], axis=0).astype(BF)
    late_copies, own_late = exchange(late_out, late_got, late_send, late_recv, 2)

    delta = d_box * (delta + d_box * dot(added.astype(BF), late[...]))
    for copy in back_copies:
        copy.wait_recv()
    own_back.wait()
    mine = [unfold(back_in[box_owner[0, 0, i]], 32) for i in range(4)]
    mine = jnp.concatenate(mine, axis=0).astype(BF)
    delta = delta + d_box * dot(mine[:, :FACES], put_face[...])
    delta = delta + dot(mine, put_mean[...])
    cells = []
    for x in range(6):
        part = [delta[i * SP : (i + 1) * SP, x * 64 : (x + 1) * 64] for i in range(4)]
        part = jnp.concatenate(part, axis=1)
        cells += [jnp.where(y_lane == y, part, 0.0) for y in range(6)]
    changes = dot(jnp.concatenate(cells, axis=0).astype(BF), give)
    rest = jnp.zeros((ROWS - 2 * SP, NZ), F32)
    for x in range(6):
        part = slice((x % 2) * SP, (x % 2 + 1) * SP)
        before = yrecv[0, x // 2].astype(F32)[part]
        after = yrecv[1, x // 2].astype(F32)[part]
        around = jnp.concatenate([before, rest, after], axis=0)
        if x == 0:
            around = around + xrecv[0].astype(F32)
        if x == 5:
            around = around + xrecv[1].astype(F32)
        change = changes[x * ROWS : (x + 1) * ROWS]
        total = adv[x] + d_slab * around + change
        if 1 <= x <= 4:
            middle = jnp.where(inside > 0, change[SP : ROWS - SP], total[SP : ROWS - SP])
            total = jnp.concatenate([total[:SP], middle, total[ROWS - SP :]], axis=0)
        ov[x] = total.reshape(6, SP, NZ)[:, :S]
        put(ov.at[x], coarse_mid.at[x], x)

    for copy in [to_right, to_left, to_down, to_up] + ghost_copies + back_copies:
        copy.wait_send()
    for copy in late_copies:
        copy.wait()
    own_late.wait()
    for copy in stores:
        copy.wait()


def finish(
    coarse_in,
    field_in,
    late_in,
    touch_in,
    diffusion_in,
    coarse_out,
    fine_out,
    diffusion,
    cells,
    field,
    late_got,
    touch,
    fv,
    load_sem,
    out_sem,
):
    pairs = [(late_in, late_got), (touch_in, touch), (field_in, field)]
    pairs += [(coarse_in.at[x], cells.at[x]) for x in range(6)]
    loads = [pltpu.make_async_copy(p[0], p[1], load_sem.at[n]) for n, p in enumerate(pairs)]
    small = pltpu.make_async_copy(diffusion_in, diffusion, load_sem.at[9])
    small.start()
    for copy in loads:
        copy.start()
    small.wait()

    d_slot = [jnp.full((8, 1), diffusion[s], F32) for s in range(S)]
    d_slot = jnp.concatenate(d_slot + [jnp.zeros((8, 1), F32)], axis=0)
    row = iota((SLOT, 8 * SP), 0)
    inward = one(iota((SLOT, 8 * SP), 1) == (row & 7) * SP + (row >> 3))
    stores = []
    for x in range(6):
        loads[3 + x].wait()
        stores.append(pltpu.make_async_copy(cells.at[x], coarse_out.at[x], out_sem.at[x]))
        stores[-1].start()

    for copy in loads[:3]:
        copy.wait()
    parts = []
    for j in range(8):
        value = late_got[j].astype(F32)
        parts += [value[:8, :64], value[:8, 64:], value[8:, :64]]
    got = dot(inward, jnp.concatenate(parts, axis=0).astype(BF)).astype(BF)
    total = field[...] + (d_slot * d_slot) * dot(got, touch[...])
    fv[...] = total[: S * 8].reshape(S, 8, FINE).astype(BF)
    stores.append(pltpu.make_async_copy(fv, fine_out, out_sem.at[6]))
    stores[-1].start()
    for copy in stores:
        copy.wait()


def local(n_gx, n_yz, consts, coarse_state, fine_state, diffusion, rate, box_pos, box_owner):
    hbm = pl.BlockSpec(memory_space=pl.ANY)
    dma = pltpu.SemaphoreType.DMA
    middle = [((6, 6, S, NZ), F32), ((SLOT, FINE), F32), ((8, 16, 128), BF)]
    between = pl.pallas_call(
        functools.partial(kernel, n_gx, n_yz),
        out_shape=tuple(jax.ShapeDtypeStruct(*m) for m in middle),
        in_specs=[hbm] * (6 + len(consts)),
        out_specs=(hbm,) * len(middle),
        scratch_shapes=[
            pltpu.SMEM((S,), F32),
            pltpu.VMEM((S, S), F32),
            pltpu.SMEM((1, 1, 4), jnp.int32),
            pltpu.SMEM((1, 1, 4), jnp.int32),
            pltpu.VMEM((6, 6, S, NZ), F32),
            pltpu.VMEM((S, 8, FINE), BF),
            *[pltpu.VMEM(c.shape, BF) for c in consts],
            pltpu.VMEM((128, 128), F32),
            pltpu.VMEM((6, ROWS, NZ), F32),
            pltpu.VMEM((6, ROWS, NZ), BF),
            pltpu.VMEM((6, ROWS, NZ), F32),
            pltpu.VMEM((2, 3, 2 * SP, NZ), BF),
            pltpu.VMEM((2, 3, 2 * SP, NZ), BF),
            pltpu.VMEM((2, ROWS, NZ), BF),
            *[pltpu.VMEM((8, 40, 128), BF)] * 2,
            *[pltpu.VMEM((8, 32, 128), BF)] * 2,
            pltpu.VMEM((8, 16, 128), BF),
            pltpu.VMEM((SLOT, FINE), F32),
            pltpu.VMEM((6, 6, S, NZ), F32),
            dma((10,)),
            dma((1 + len(consts),)),
            dma((3,)),
            dma((4,)),
            dma((4,)),
            *[dma((8,))] * 6,
            dma((11,)),
            pltpu.SemaphoreType.REGULAR,
        ],
        compiler_params=pltpu.CompilerParams(
            collective_id=0, has_side_effects=True, vmem_limit_bytes=56 * 1024 * 1024
        ),
        name="amr_step",
    )(
        jnp.transpose(coarse_state, (1, 2, 0, 3)),
        jnp.transpose(fine_state, (1, 0, 2)),
        diffusion,
        rate,
        box_pos,
        box_owner,
        *consts,
    )
    last = consts[1][:64, :FINE]
    coarse, fine = pl.pallas_call(
        finish,
        out_shape=(
            jax.ShapeDtypeStruct((6, 6, S, NZ), F32),
            jax.ShapeDtypeStruct((S, 8, FINE), BF),
        ),
        in_specs=[hbm] * (len(middle) + 2),
        out_specs=(hbm, hbm),
        scratch_shapes=[
            pltpu.SMEM((S,), F32),
            *[pltpu.VMEM(*m) for m in middle],
            pltpu.VMEM(last.shape, BF),
            pltpu.VMEM((S, 8, FINE), BF),
            dma((10,)),
            dma((7,)),
        ],
        compiler_params=pltpu.CompilerParams(vmem_limit_bytes=56 * 1024 * 1024),
        name="finish",
    )(*between, last, diffusion)
    return jnp.transpose(coarse, (2, 0, 1, 3)), jnp.transpose(fine, (1, 0, 2))


def solution(mesh):
    in_specs = (
        P(None, "gx", "yz", None),
        P(("gx", "yz"), None, None),
        P(),
        P(),
        P("gx", "yz", None),
        P("gx", "yz", None),
    )
    out_specs = (P(None, "gx", "yz", None), P(("gx", "yz"), None, None))
    consts = [np.asarray(c).astype(jnp.bfloat16) for c in constants()]
    body = functools.partial(local, mesh.shape["gx"], mesh.shape["yz"], consts)
    return jax.shard_map(body, mesh=mesh, in_specs=in_specs, out_specs=out_specs, check_vma=False)
```

```python
import functools

import jax
import jax.numpy as jnp
import numpy as np
from jax import lax
from jax.experimental import pallas as pl
from jax.experimental.pallas import tpu as pltpu
from jax.sharding import PartitionSpec as P

S = 21
BF = jnp.bfloat16
F32 = jnp.float32
SP = 24
ROWS = 6 * SP
NZ = 384
PATCH = 384
FINE = 512
SLOT = 176
FACES = 128
FLAG = 21


def constants():
    def patch(at):
        return at[0] * 64 + at[1] * 8 + at[2]

    faces = []
    for axis in range(3):
        for low, inner in ((0, 1), (5, 4)):
            for a in range(1, 5):
                for b in range(1, 5):
                    at, near = [a, b], [a, b]
                    at.insert(axis, low)
                    near.insert(axis, inner)
                    faces.append((tuple(at), tuple(near), axis))
    number = {at: n for n, (at, _, _) in enumerate(faces)}
    touch = np.zeros((FACES, FINE), np.float32)
    lap = np.zeros((FINE, FINE), np.float32)
    mean = np.zeros((FINE, 256), np.float32)
    put_mean = np.zeros((256, PATCH), np.float32)
    cells = [(x, y, z) for x in range(8) for y in range(8) for z in range(8)]
    for cell, at in enumerate(cells):
        lap[cell, cell] = -6.0
        inner = [c // 2 + 1 for c in at]
        box = 96 + (inner[0] - 1) * 16 + (inner[1] - 1) * 4 + inner[2] - 1
        mean[cell, box] = 0.125
        put_mean[box, patch(inner)] = 1.0
        for axis, stride in enumerate((64, 8, 1)):
            for step, edge, ghost in ((-1, 0, 0), (1, 7, 5)):
                if at[axis] == edge:
                    cyc = list(inner)
                    cyc[axis] = ghost
                    touch[number[tuple(cyc)], cell] = 1.0
                else:
                    lap[cell + step * stride, cell] = 1.0
    lap_pool = np.concatenate([lap, 0.25 * touch.T], axis=1)
    ghosts = np.zeros((2 * PATCH, 2 * FACES), np.float32)
    fixes = np.zeros((2 * PATCH, PATCH), np.float32)
    put_face = np.zeros((FACES, PATCH), np.float32)
    sides = np.zeros((256, FACES), np.float32)
    for n, (at, near, axis) in enumerate(faces):
        q = patch(at)
        ghosts[q, n] = 1.0
        ghosts[PATCH + q, 96 + n] = 1.0
        fixes[q, q] = 1.0 - 1.5
        fixes[patch(near), q] = -1.0
        fixes[PATCH + q, q] = -0.5
        put_face[n, q] = 1.0
        if n < 64:
            rest = [at[d] for d in range(3) if d != axis]
            sides[n // 16 * 64 + rest[0] * 8 + rest[1], n] = 1.0
    late = (touch @ mean @ put_mean) - 0.5 * put_face
    late[64:] = 0.0
    both = np.zeros((2 * FACES, 2 * FINE), np.float32)
    both[:96, :FINE] = touch[:96]
    both[96:192, FINE:] = touch[:96]
    return (lap_pool, both, mean, ghosts, fixes, put_face, put_mean, sides, late)


def iota(shape, dim):
    return lax.broadcasted_iota(jnp.int32, shape, dim)


def dot(a, b):
    return jnp.dot(a, b, preferred_element_type=F32)


def dot_nt(a, b):
    return lax.dot_general(a, b, (((1,), (1,)), ((), ())), preferred_element_type=F32)


def one(mask, kind=BF):
    return jnp.where(mask, 1.0, 0.0).astype(kind)


def split(value):
    high = value.astype(BF)
    return high, (value - high.astype(F32)).astype(BF)


def fold(value, width):
    tiles = [value[n : n + 8, 128 : 128 + width] for n in range(0, SP, 8)]
    if width == 32:
        tiles = [jnp.concatenate(tiles + [jnp.zeros((8, 32), F32)], axis=1)]
    else:
        tiles = [
            jnp.concatenate(tiles[:2], axis=1),
            jnp.concatenate([tiles[2], jnp.zeros((8, 64), F32)], axis=1),
        ]
    return jnp.concatenate([value[:, :128]] + tiles, axis=0)


def unfold(value, width):
    value = value.astype(F32)
    if width == 32:
        tiles = [value[SP:, n * 32 : (n + 1) * 32] for n in range(3)]
    else:
        tiles = [value[SP : SP + 8, :64], value[SP : SP + 8, 64:], value[SP + 8 :, :64]]
    rest = jnp.concatenate([jnp.concatenate(tiles, axis=0), jnp.zeros((SP, 128 - width), F32)], axis=1)
    return jnp.concatenate([value[:SP], rest], axis=1)


def kernel(
    n_gx,
    n_yz,
    coarse,
    fine,
    diffusion_in,
    rate_in,
    box_pos_in,
    box_owner_in,
    lap_pool_in,
    touch_in,
    mean_in,
    ghosts_in,
    fixes_in,
    put_face_in,
    put_mean_in,
    sides_in,
    late_in,
    coarse_mid,
    field_out,
    late_got,
    diffusion,
    rate,
    box_pos,
    box_owner,
    cv,
    fv,
    lap_pool,
    touch,
    mean,
    ghosts,
    fixes,
    put_face,
    put_mean,
    sides,
    late,
    rz,
    xf,
    xh,
    adv,
    ysend,
    yrecv,
    xrecv,
    ghost_out,
    ghost_in,
    back_out,
    back_in,
    late_out,
    field_tmp,
    ov,
    plane_sem,
    load_sem,
    own_sem,
    halo_send,
    halo_recv,
    ghost_send,
    ghost_recv,
    back_send,
    back_recv,
    late_send,
    late_recv,
    out_sem,
    ready,
):
    gx = lax.axis_index("gx")
    me = lax.axis_index("yz")
    right, left = lax.rem(gx + 1, n_gx), lax.rem(gx + n_gx - 1, n_gx)
    up, down = lax.rem(me + 1, n_yz), lax.rem(me + n_yz - 1, n_yz)
    mesh_id = pl.DeviceIdType.MESH

    planes = [pltpu.make_async_copy(coarse.at[x], cv.at[x], plane_sem.at[x]) for x in range(6)]
    planes[5].start()

    barrier = pltpu.get_barrier_semaphore()
    for step in range(1, n_yz):
        pl.semaphore_signal(
            barrier, inc=1, device_id=(gx, lax.rem(me + step, n_yz)), device_id_type=mesh_id
        )
    pl.semaphore_signal(barrier, inc=1, device_id=(left, me), device_id_type=mesh_id)

    small = [
        (rate_in, rate),
        (diffusion_in, diffusion),
        (box_pos_in, box_pos),
        (box_owner_in, box_owner),
    ]
    small = [pltpu.make_async_copy(p[0], p[1], plane_sem.at[6 + n]) for n, p in enumerate(small)]
    for copy in small + planes[:5]:
        copy.start()
    loads = [
        pltpu.make_async_copy(src, dst, load_sem.at[n])
        for n, (src, dst) in enumerate(
            [
                (fine, fv),
                (lap_pool_in, lap_pool),
                (touch_in, touch),
                (mean_in, mean),
                (ghosts_in, ghosts),
                (fixes_in, fixes),
                (put_face_in, put_face),
                (put_mean_in, put_mean),
                (sides_in, sides),
                (late_in, late),
            ]
        )
    ]
    for copy in loads:
        copy.start()

    def remote(src, dst, sends, recvs, at, target):
        return pltpu.make_async_remote_copy(
            src_ref=src,
            dst_ref=dst,
            send_sem=sends.at[at],
            recv_sem=recvs.at[at],
            device_id=target,
            device_id_type=mesh_id,
        )

    def exchange(out, got, sends, recvs, n):
        copies = []
        for step in (4, 3, 5, 2, 6, 1, 7):
            other = lax.rem(me + step, n_yz)
            copies.append(remote(out.at[other], got.at[me], sends, recvs, step, (gx, other)))
            copies[-1].start()
        own = pltpu.make_async_copy(out.at[me], got.at[me], own_sem.at[n])
        own.start()
        return copies, own

    def slab(x):
        planes[x].wait()
        value = jnp.concatenate([cv[x], jnp.zeros((6, SP - S, NZ), F32)], axis=1)
        value = value.reshape(ROWS, NZ)
        xf[x] = value
        xh[x] = value.astype(BF)

    to_right = remote(xh.at[5], xrecv.at[0], halo_send, halo_recv, 0, (right, me))
    to_left = remote(xh.at[0], xrecv.at[1], halo_send, halo_recv, 1, (left, me))
    to_down = remote(ysend.at[0], yrecv.at[1], halo_send, halo_recv, 2, (gx, down))
    to_up = remote(ysend.at[1], yrecv.at[0], halo_send, halo_recv, 3, (gx, up))
    slab(5)

    def enter():
        pl.semaphore_wait(barrier, n_yz)
        to_right.start()
        pl.semaphore_signal(ready, inc=1, device_id=(right, me), device_id_type=mesh_id)

    pl.when(gx == n_gx - 1)(enter)
    for x in range(5):
        slab(x)
    for pair in range(3):
        for side, part in ((0, slice(0, SP)), (1, slice(ROWS - SP, ROWS))):
            layers = [xf[2 * pair, part], xf[2 * pair + 1, part]]
            ysend[side, pair] = jnp.concatenate(layers, axis=0).astype(BF)
    for copy in small:
        copy.wait()
    rz[...] = jnp.zeros_like(rz)
    rz[0:S, 0:S] = rate[...]
    rate_high, rate_low = split(rz[...])
    tall = one(iota((6, SP, 128), 1) == iota((6, SP, 128), 2), F32)
    tall = tall.reshape(ROWS, 128).astype(BF)
    y_row = iota((6, SP, 1), 0).astype(F32).reshape(ROWS, 1)
    lane = iota((1, ROWS), 1)
    y_col = jnp.zeros((1, ROWS), F32)
    for y in range(1, 6):
        y_col = y_col + jnp.where(lane >= y * SP, 1.0, 0.0)

    def mix(part):
        full = dot_nt(dot(tall, part).astype(BF), tall)
        return jnp.where(y_row == y_col, full, 0.0).astype(BF)

    mix_high = mix(rate_high)
    mix_both = jnp.concatenate([mix_high, mix(rate_low)], axis=0)
    at = iota((SP, 1), 0)
    column = jnp.zeros((SP, 1), F32)
    for s in range(S):
        column = jnp.where(at == s, diffusion[s], column)
    d_slab = jnp.concatenate([column] * 6, axis=0)
    d_box = jnp.concatenate([column] * 4, axis=0)

    def start_of(index):
        place = jnp.full(index.shape, box_pos[0, 0, 0] * 6, jnp.int32)
        for i in range(1, 4):
            place = jnp.where(index == i, box_pos[0, 0, i] * 6, place)
        return place

    lane = iota((1, 256), 1)
    want = jnp.where((lane & 7) < 6, start_of(lane >> 6) + (lane & 7), -1)
    take = one(iota((NZ, 256), 0) == want)
    y_lane = (iota((1, 256), 1) >> 3) & 7

    def to_patches(slabs):
        cells = dot(jnp.concatenate(slabs, axis=0), take)
        patches = []
        for n in range(0, ROWS * len(slabs), ROWS):
            patch = jnp.zeros((SP, 256), F32)
            for y in range(6):
                patch = jnp.where(y_lane == y, cells[n + y * SP : n + (y + 1) * SP], patch)
            patches.append(patch)
        return patches

    def by_box(parts):
        rows = [
            jnp.concatenate([part[:, i * 64 : (i + 1) * 64] for part in parts], axis=1)
            for i in range(4)
        ]
        return jnp.concatenate(rows, axis=0)

    def for_owner(value, owner):
        total = jnp.zeros((SP, value.shape[1]), F32)
        for i in range(4):
            sent = box_owner[0, 0, i] == owner
            total = total + jnp.where(sent, value[i * SP : (i + 1) * SP], 0.0)
        return total

    stores = []

    def put(src, dst, n):
        stores.append(pltpu.make_async_copy(src, dst, out_sem.at[n]))
        stores[-1].start()

    news = []
    for x in range(6):
        value = xf[x]
        high = xh[x]
        low = (value - high.astype(F32)).astype(BF)
        around = pltpu.roll(value, 1, 1) + pltpu.roll(value, NZ - 1, 1) - 6.0 * value
        if x > 0:
            around = around + xf[x - 1]
        if x < 5:
            around = around + xf[x + 1]
        rest = jnp.zeros((SP, NZ), F32)
        around = around + jnp.concatenate([rest, value[: ROWS - SP]], axis=0)
        around = around + jnp.concatenate([value[SP:], rest], axis=0)
        mixed = dot(mix_both, high)
        mixed = mixed[:ROWS] + mixed[ROWS:] + dot(mix_high, low)
        value = value + mixed + d_slab * around
        adv[x] = value
        news.append(value.astype(BF))
    olds = by_box(to_patches([xh[x] for x in range(6)]))
    patches = jnp.concatenate([olds, by_box(to_patches(news))], axis=1).astype(BF)
    for n in (4, 5):
        loads[n].wait()
    sent = dot(patches, ghosts[...])
    flag = jnp.concatenate([one(at == FLAG, F32)] * 4, axis=0)
    sent = sent + flag
    for owner in range(8):
        ghost_out[owner] = fold(for_owner(sent, owner), 64).astype(BF)
    pl.when(gx != n_gx - 1)(enter)
    ghost_copies, own_ghost = exchange(ghost_out, ghost_in, ghost_send, ghost_recv, 0)
    to_down.start()
    to_up.start()

    @pl.when(gx > 1)
    def _():
        pl.semaphore_wait(ready, 1)
        to_left.start()


    for n in (0, 1, 2, 3):
        loads[n].wait()
    field = fv[...].astype(F32).reshape(S * 8, FINE)
    field = jnp.concatenate([field, jnp.zeros((8, FINE), F32)], axis=0)
    tall = one((iota((SLOT, 128), 0) >> 3) == iota((SLOT, 128), 1))
    slot_same = (iota((SLOT, SLOT), 0) & 7) == (iota((SLOT, SLOT), 1) & 7)

    def slot_rate(part):
        full = dot_nt(dot(tall, part).astype(BF), tall)
        return jnp.where(slot_same, 0.5 * full, 0.0).astype(BF)

    slot_high = slot_rate(rate_high)
    slot_both = jnp.concatenate([slot_high, slot_rate(rate_low)], axis=0)
    d_slot = [jnp.full((8, 1), diffusion[s], F32) for s in range(S)]
    d_slot = jnp.concatenate(d_slot + [jnp.zeros((8, 1), F32)], axis=0)
    row = iota((SLOT, 8 * SP), 0)
    inward = one(iota((SLOT, 8 * SP), 1) == (row & 7) * SP + (row >> 3))
    row = iota((8, SP, SLOT), 1) * 8 + iota((8, SP, SLOT), 0)
    outward = (row == iota((8, SP, SLOT), 2)) & (iota((8, SP, SLOT), 1) < S)
    outward = one(outward, F32).reshape(8 * SP, SLOT).astype(BF)
    high = field.astype(BF)
    both = dot(high, lap_pool[...])
    mixed = dot(slot_both, high)
    pooled = both[:, FINE:]
    field = (
        field + (2.0 * d_slot) * both[:, :FINE] + mixed[:SLOT] + mixed[SLOT:]
    )

    for copy in ghost_copies:
        copy.wait_recv()
    own_ghost.wait()

    got = jnp.concatenate([unfold(ghost_in[j], 64) for j in range(8)], axis=0).astype(BF)
    got = dot(inward, got)
    used = jnp.concatenate([got[S * 8 :, 0:1]] * (SLOT // 8), axis=0) > 0.5
    got = got.astype(BF)
    spread = dot(got, touch[...])
    ghost_old = spread[:, :FINE]
    ghost_mid = 0.5 * (ghost_old + spread[:, FINE:])
    field = field + (2.0 * d_slot) * ghost_old
    high, low = split(field)
    both = dot(jnp.concatenate([high, low], axis=0), lap_pool[...])
    both = both[:SLOT] + both[SLOT:]
    mixed = dot(slot_both, high)
    pooled = pooled + both[:, FINE:]
    field = (
        field
        + (2.0 * d_slot) * (both[:, :FINE] + ghost_mid)
        + (mixed[:SLOT] + mixed[SLOT:] + dot(slot_high, low))
    )
    field_tmp[...] = jnp.where(used, field, 0.0)
    back = dot(field.astype(BF), mean[...])
    back = jnp.concatenate([back[:, :FACES] + pooled, back[:, FACES:]], axis=1)
    back = dot(outward, back.astype(BF))
    for host in range(8):
        back_out[host] = fold(back[host * SP : (host + 1) * SP], 32).astype(BF)
    back_copies, own_back = exchange(back_out, back_in, back_send, back_recv, 1)

    put(field_tmp, field_out, 6)

    lane = iota((256, 1), 0)
    want = jnp.where((lane & 7) < 6, start_of(lane >> 6) + (lane & 7), -1)
    give = one(iota((256, NZ), 1) == want)
    zat = iota((1, NZ), 1)
    inside = jnp.zeros((1, NZ), jnp.int32)
    for i in range(4):
        offset = zat - box_pos[0, 0, i] * 6
        inside = inside + jnp.where((offset >= 1) & (offset <= 4), 1, 0)

    for n in (6, 7, 8, 9):
        loads[n].wait()
    delta = dot(patches, fixes[...])
    to_down.wait_recv()
    to_up.wait_recv()
    layers = [jnp.concatenate([yrecv[n, pair] for pair in range(3)], axis=0) for n in range(2)]
    to_left.wait_recv()
    parts = to_patches([xrecv[1]] + layers)
    to_right.wait_recv()
    parts = to_patches([xrecv[0]]) + parts
    added = by_box(parts).astype(BF)
    added = dot(added, sides[...])
    for owner in range(8):
        part = for_owner(added, owner)
        first = jnp.concatenate([part[0:8, :64], part[8:16, :64]], axis=1)
        last = jnp.concatenate([part[16:24, :64], jnp.zeros((8, 64), F32)], axis=1)
        late_out[owner] = jnp.concatenate([first, last], axis=0).astype(BF)
    late_copies, own_late = exchange(late_out, late_got, late_send, late_recv, 2)

    @pl.when(gx <= 1)
    def _():
        pl.semaphore_wait(ready, 1)
        to_left.start()

    delta = d_box * (delta + d_box * dot(added.astype(BF), late[...]))
    for copy in back_copies:
        copy.wait_recv()
    own_back.wait()
    mine = [unfold(back_in[box_owner[0, 0, i]], 32) for i in range(4)]
    mine = jnp.concatenate(mine, axis=0).astype(BF)
    delta = delta + d_box * dot(mine[:, :FACES], put_face[...])
    delta = delta + dot(mine, put_mean[...])
    cells = []
    for x in range(6):
        part = [delta[i * SP : (i + 1) * SP, x * 64 : (x + 1) * 64] for i in range(4)]
        part = jnp.concatenate(part, axis=1)
        cells += [jnp.where(y_lane == y, part, 0.0) for y in range(6)]
    changes = dot(jnp.concatenate(cells, axis=0).astype(BF), give)
    rest = jnp.zeros((ROWS - 2 * SP, NZ), F32)
    for x in range(6):
        part = slice((x % 2) * SP, (x % 2 + 1) * SP)
        before = yrecv[0, x // 2].astype(F32)[part]
        after = yrecv[1, x // 2].astype(F32)[part]
        around = jnp.concatenate([before, rest, after], axis=0)
        if x == 0:
            around = around + xrecv[0].astype(F32)
        if x == 5:
            around = around + xrecv[1].astype(F32)
        change = changes[x * ROWS : (x + 1) * ROWS]
        total = adv[x] + d_slab * around + change
        if 1 <= x <= 4:
            middle = jnp.where(inside > 0, change[SP : ROWS - SP], total[SP : ROWS - SP])
            total = jnp.concatenate([total[:SP], middle, total[ROWS - SP :]], axis=0)
        ov[x] = total.reshape(6, SP, NZ)[:, :S]
        put(ov.at[x], coarse_mid.at[x], x)

    for copy in [to_right, to_left, to_down, to_up] + ghost_copies + back_copies:
        copy.wait_send()
    for copy in late_copies:
        copy.wait()
    own_late.wait()
    for copy in stores:
        copy.wait()


def finish(
    coarse_in,
    field_in,
    late_in,
    touch_in,
    diffusion_in,
    coarse_out,
    fine_out,
    diffusion,
    cells,
    field,
    late_got,
    touch,
    fv,
    load_sem,
    out_sem,
):
    pairs = [(late_in, late_got), (touch_in, touch), (field_in, field)]
    pairs += [(coarse_in.at[x], cells.at[x]) for x in range(6)]
    loads = [pltpu.make_async_copy(p[0], p[1], load_sem.at[n]) for n, p in enumerate(pairs)]
    small = pltpu.make_async_copy(diffusion_in, diffusion, load_sem.at[9])
    small.start()
    for copy in loads:
        copy.start()
    small.wait()

    d_slot = [jnp.full((8, 1), diffusion[s], F32) for s in range(S)]
    d_slot = jnp.concatenate(d_slot + [jnp.zeros((8, 1), F32)], axis=0)
    row = iota((SLOT, 8 * SP), 0)
    inward = one(iota((SLOT, 8 * SP), 1) == (row & 7) * SP + (row >> 3))
    stores = []
    for x in range(6):
        loads[3 + x].wait()
        stores.append(pltpu.make_async_copy(cells.at[x], coarse_out.at[x], out_sem.at[x]))
        stores[-1].start()

    for copy in loads[:3]:
        copy.wait()
    parts = []
    for j in range(8):
        value = late_got[j].astype(F32)
        parts += [value[:8, :64], value[:8, 64:], value[8:, :64]]
    got = dot(inward, jnp.concatenate(parts, axis=0).astype(BF)).astype(BF)
    total = field[...] + (d_slot * d_slot) * dot(got, touch[...])
    fv[...] = total[: S * 8].reshape(S, 8, FINE).astype(BF)
    stores.append(pltpu.make_async_copy(fv, fine_out, out_sem.at[6]))
    stores[-1].start()
    for copy in stores:
        copy.wait()


def local(n_gx, n_yz, consts, coarse_state, fine_state, diffusion, rate, box_pos, box_owner):
    hbm = pl.BlockSpec(memory_space=pl.ANY)
    dma = pltpu.SemaphoreType.DMA
    middle = [((6, 6, S, NZ), F32), ((SLOT, FINE), F32), ((8, 16, 128), BF)]
    between = pl.pallas_call(
        functools.partial(kernel, n_gx, n_yz),
        out_shape=tuple(jax.ShapeDtypeStruct(*m) for m in middle),
        in_specs=[hbm] * (6 + len(consts)),
        out_specs=(hbm,) * len(middle),
        scratch_shapes=[
            pltpu.SMEM((S,), F32),
            pltpu.VMEM((S, S), F32),
            pltpu.SMEM((1, 1, 4), jnp.int32),
            pltpu.SMEM((1, 1, 4), jnp.int32),
            pltpu.VMEM((6, 6, S, NZ), F32),
            pltpu.VMEM((S, 8, FINE), BF),
            *[pltpu.VMEM(c.shape, BF) for c in consts],
            pltpu.VMEM((128, 128), F32),
            pltpu.VMEM((6, ROWS, NZ), F32),
            pltpu.VMEM((6, ROWS, NZ), BF),
            pltpu.VMEM((6, ROWS, NZ), F32),
            pltpu.VMEM((2, 3, 2 * SP, NZ), BF),
            pltpu.VMEM((2, 3, 2 * SP, NZ), BF),
            pltpu.VMEM((2, ROWS, NZ), BF),
            *[pltpu.VMEM((8, 40, 128), BF)] * 2,
            *[pltpu.VMEM((8, 32, 128), BF)] * 2,
            pltpu.VMEM((8, 16, 128), BF),
            pltpu.VMEM((SLOT, FINE), F32),
            pltpu.VMEM((6, 6, S, NZ), F32),
            dma((10,)),
            dma((1 + len(consts),)),
            dma((3,)),
            dma((4,)),
            dma((4,)),
            *[dma((8,))] * 6,
            dma((11,)),
            pltpu.SemaphoreType.REGULAR,
        ],
        compiler_params=pltpu.CompilerParams(
            collective_id=0, has_side_effects=True, vmem_limit_bytes=56 * 1024 * 1024
        ),
        name="amr_step",
    )(
        jnp.transpose(coarse_state, (1, 2, 0, 3)),
        jnp.transpose(fine_state, (1, 0, 2)),
        diffusion,
        rate,
        box_pos,
        box_owner,
        *consts,
    )
    last = consts[1][:64, :FINE]
    coarse, fine = pl.pallas_call(
        finish,
        out_shape=(
            jax.ShapeDtypeStruct((6, 6, S, NZ), F32),
            jax.ShapeDtypeStruct((S, 8, FINE), BF),
        ),
        in_specs=[hbm] * (len(middle) + 2),
        out_specs=(hbm, hbm),
        scratch_shapes=[
            pltpu.SMEM((S,), F32),
            *[pltpu.VMEM(*m) for m in middle],
            pltpu.VMEM(last.shape, BF),
            pltpu.VMEM((S, 8, FINE), BF),
            dma((10,)),
            dma((7,)),
        ],
        compiler_params=pltpu.CompilerParams(vmem_limit_bytes=56 * 1024 * 1024),
        name="finish",
    )(*between, last, diffusion)
    return jnp.transpose(coarse, (2, 0, 1, 3)), jnp.transpose(fine, (1, 0, 2))


def solution(mesh):
    in_specs = (
        P(None, "gx", "yz", None),
        P(("gx", "yz"), None, None),
        P(),
        P(),
        P("gx", "yz", None),
        P("gx", "yz", None),
    )
    out_specs = (P(None, "gx", "yz", None), P(("gx", "yz"), None, None))
    consts = [np.asarray(c).astype(jnp.bfloat16) for c in constants()]
    body = functools.partial(local, mesh.shape["gx"], mesh.shape["yz"], consts)
    return jax.shard_map(body, mesh=mesh, in_specs=in_specs, out_specs=out_specs, check_vma=False)
```
